32 devices in a mesh: row: 8 (over y, x, core), col: 4 (over z).
Axes of the slice: x: 2, y: 2, z: 4, core: 2. Of those that a mesh axis runs over, the one named last changes fastest.
Arguments:
- amplitudes: bfloat16 [1280, 3, 256], P(('row', 'col')), may hold values from -6 to 6
- integrals: bfloat16 [3, 256, 65536], P(None, 'row', 'col'), may hold values from -0.625 to 0.625
- pair_irrep: int32 [3, 256], replicated, may hold values from 0 to 8
- block_offset: int32 [9], replicated, may hold values from 0 to 65536, as said below
- residual: bfloat16 [1280, 65536], P(('row', 'col')), may hold values from -6 to 6
Outputs:
- residual_out: bfloat16 [1280, 65536], P(('row', 'col'))
The draws below stay inside these ranges and needn't reach their ends.
Inputs may be any that keep to these rules, and one draw needn't show every extreme that they name: block_offset[0] is 0 and block_offset[8] is 65536; the entries rise strictly and are multiples of 128.
All inputs are finite; a program needn't handle non-finite values.
Results may differ from the reference program's by a relative error of at most 0.0043.
Values may be sent and summed in bfloat16 or wider, within the bound.
A program may use at most 192 MiB of HBM per device.

```python
import jax
import jax.numpy as jnp
from jax import lax

NIRREP = 8
PADGRAIN = 128
PANEL = 256
STEPS = 3
OPAIRS = 1280
VPAIRS = 65536
N_ROW = 8


def draw_block_offset(key, part):
    key = jax.random.fold_in(key, 11)
    units = VPAIRS // PADGRAIN
    reach = units // (4 * NIRREP)
    extra = jax.random.randint(key, (NIRREP,), 0, reach + 1)
    sizes = units // NIRREP + extra - jnp.roll(extra, -1)
    ends = jnp.cumsum(sizes) * PADGRAIN
    ends = ends.at[NIRREP - 1].set(VPAIRS)
    return jnp.concatenate([jnp.zeros((1,), jnp.int32), ends.astype(jnp.int32)])


def with_ends(array, stream_key, least, high):
    index_at = [jax.random.randint(jax.random.fold_in(stream_key, axis), (), 0, length) for axis, length in enumerate(array.shape)]
    widest = array.shape.index(max(array.shape))
    next_to = index_at[:widest] + [(index_at[widest] + 1) % array.shape[widest]] + index_at[widest + 1:]
    return array.at[tuple(index_at)].set(least).at[tuple(next_to)].set(high)


def level_of(rng, shape, pieces, least, largest):
    gain = 1.0
    for dim, shards_of in pieces:
        draws = jax.random.uniform(jax.random.fold_in(jax.random.fold_in(rng, 6), dim), (shards_of,), jnp.float32, least / len(pieces), largest / len(pieces))
        gain = gain * jnp.repeat(jnp.exp(draws), shape[dim] // shards_of).reshape((-1,) + (1,) * (len(shape) - 1 - dim))
    return gain


def bell_draw(rng, shape, spread, most, shards=(), kind=jnp.bfloat16):
    array = jax.random.normal(rng, shape, jnp.float32) * spread
    if len(shards) > 0:
        array = level_of(rng, shape, shards, -0.22, 0.18) * array
    return jnp.clip(array, min=-most, max=most).astype(kind)


def setup_inputs(seed: int = 0) -> dict:
    arg_keys = jax.random.split(jax.random.key(seed), 6)
    amplitudes = bell_draw(arg_keys[0], (OPAIRS, STEPS, PANEL), 1.0, 6.0, ((0, 32),))
    integrals = bell_draw(arg_keys[1], (STEPS, PANEL, VPAIRS), (STEPS * PANEL // (NIRREP + 1)) ** -0.5, 0.625, ((1, 8), (2, 4)))
    pair_irrep = with_ends(jax.random.randint(arg_keys[2], (STEPS, PANEL), 0, NIRREP + 1), jax.random.fold_in(arg_keys[2], 1), 0, NIRREP).astype(jnp.int32)
    block_offset = draw_block_offset(jax.random.fold_in(arg_keys[5], 71), 0)
    residual = bell_draw(arg_keys[4], (OPAIRS, VPAIRS), 1.0, 6.0, ((0, 32),))
    return dict(amplitudes=amplitudes, integrals=integrals, pair_irrep=pair_irrep, block_offset=block_offset, residual=residual)


def reference(amplitudes, integrals, pair_irrep, block_offset, residual):
    position = jnp.arange(VPAIRS, dtype=jnp.int32)
    irrep_ab = jnp.sum((position[:, None] >= block_offset[None, 1:-1]).astype(jnp.int32), axis=1).astype(jnp.int32)
    masked = jnp.where(pair_irrep[:, :, None] == irrep_ab[None, None, :], integrals, jnp.zeros((), integrals.dtype))
    masked_wide = masked.reshape(STEPS * PANEL, VPAIRS).astype(jnp.float32)
    amp_wide = amplitudes.reshape(N_ROW, OPAIRS // N_ROW, STEPS * PANEL)
    res_wide = residual.reshape(N_ROW, OPAIRS // N_ROW, VPAIRS)

    def one_block(pair_args):
        amp_block, res_block = pair_args
        ladder = jnp.dot(amp_block.astype(jnp.float32), masked_wide, precision=lax.Precision.HIGHEST, preferred_element_type=jnp.float32).astype(jnp.bfloat16)
        ladder = lax.optimization_barrier(ladder)
        return (res_block.astype(jnp.float32) + ladder.astype(jnp.float32)).astype(jnp.bfloat16)

    result = lax.map(one_block, (amp_wide, res_wide))
    return result.reshape(OPAIRS, VPAIRS)
```

```python
import functools

import jax
import jax.numpy as jnp
from jax import lax
from jax.experimental import pallas as pl
from jax.experimental.pallas import tpu as pltpu
from jax.sharding import PartitionSpec as P

NIRREP = 8
GRAIN = 128
MIB = 1024 * 1024


def apply_piece(irrep_ab, amp_panel, labels, total, piece):
    kept = jnp.where(labels[:, None] == irrep_ab[None, :], piece, jnp.zeros((), piece.dtype))
    return total + jnp.dot(amp_panel, kept, preferred_element_type=jnp.float32)


def dense(amplitudes, integrals, pair_irrep, block_offset, residual):
    ab_local = integrals.shape[2]
    steps = integrals.shape[0]
    position = lax.axis_index("col") * ab_local + lax.iota(jnp.int32, ab_local)
    irrep_ab = jnp.sum((position[:, None] >= block_offset[None, 1:-1]).astype(jnp.int32), axis=1)
    grid_amps = lax.all_to_all(amplitudes, "col", split_axis=2, concat_axis=0, tiled=True)
    panels = [
        lax.all_gather(grid_amps[:, step, :], "col", axis=1, tiled=True) for step in range(steps)
    ]
    total = jnp.zeros((panels[0].shape[0], ab_local), jnp.float32)
    piece = lax.all_gather(integrals, "row", axis=1, tiled=True)
    for step in range(steps):
        total = apply_piece(irrep_ab, panels[step], pair_irrep[step], total, piece[step])
    ladder_half = total.astype(jnp.bfloat16)
    returned = lax.all_to_all(ladder_half, "col", split_axis=0, concat_axis=1, tiled=True)
    return (residual.astype(jnp.float32) + returned.astype(jnp.float32)).astype(jnp.bfloat16)


def round_up(value, grain):
    return (value + grain - 1) // grain * grain


def one_hot_rows(slot_ref, g, rows):
    width = slot_ref.shape[1]
    line = slot_ref[pl.ds(g, 1), :]
    at = lax.broadcasted_iota(jnp.int32, (rows, width), 0)
    return jnp.where(line == at, 1.0, 0.0).astype(jnp.bfloat16)


def pack_kernel(irrep_ref, slot_ref, x_ref, out_ref, pick, *, blocks, per_step):
    rows = pick.shape[1]

    @pl.when(pl.program_id(0) == 0)
    def _():
        for g in range(NIRREP):
            pick[g] = one_hot_rows(slot_ref, g, rows)

    x = x_ref[...].reshape(-1, x_ref.shape[-1])
    first = irrep_ref[blocks] + pl.program_id(0) * per_step
    for t in range(per_step):
        g = irrep_ref[first + t]
        cols = slice(t * GRAIN, (t + 1) * GRAIN)
        packed = jnp.dot(pick[g], x[:, cols], preferred_element_type=jnp.float32)
        out_ref[0, :, cols] = packed.astype(jnp.bfloat16)


def pack(x, slot, irrep_blk, first, rows, parts):
    width = x.shape[-1] // parts
    depth = slot.shape[1]
    blocks = irrep_blk.shape[0]
    scalars = jnp.concatenate([irrep_blk, first[None].astype(jnp.int32)])
    lead = x.ndim - 1
    return pl.pallas_call(
        functools.partial(pack_kernel, blocks=blocks, per_step=width // GRAIN),
        out_shape=jax.ShapeDtypeStruct((parts, rows, width), jnp.bfloat16),
        grid_spec=pltpu.PrefetchScalarGridSpec(
            num_scalar_prefetch=1,
            grid=(parts,),
            in_specs=[
                pl.BlockSpec((NIRREP, depth), lambda i, s: (0, 0)),
                pl.BlockSpec(x.shape[:-1] + (width,), lambda i, s: (0,) * lead + (i,)),
            ],
            out_specs=pl.BlockSpec((1, rows, width), lambda i, s: (i, 0, 0)),
            scratch_shapes=[pltpu.VMEM((NIRREP, rows, depth), jnp.bfloat16)],
        ),
        compiler_params=pltpu.CompilerParams(vmem_limit_bytes=24 * MIB),
    )(scalars, slot, x)


def ladder_kernel(irrep_ref, slot_ref, amp_ref, packed_ref, res_ref, out_ref, amps, *, per_step):
    rows = amps.shape[2]

    @pl.when(pl.program_id(0) == 0)
    def _():
        for g in range(NIRREP):
            pick = one_hot_rows(slot_ref, g, rows)
            amps[g] = lax.dot_general(
                amp_ref[...], pick, (((1,), (1,)), ((), ())), preferred_element_type=jnp.float32
            ).astype(jnp.bfloat16)

    first = pl.program_id(0) * per_step
    for t in range(per_step):
        g = irrep_ref[first + t]
        cols = slice(t * GRAIN, (t + 1) * GRAIN)
        ladder = jnp.dot(amps[g], packed_ref[0, :, cols], preferred_element_type=jnp.float32)
        ladder = ladder.astype(jnp.bfloat16).astype(jnp.float32)
        out_ref[:, cols] = (res_ref[:, cols].astype(jnp.float32) + ladder).astype(jnp.bfloat16)


def ladder_add(amp, slot, irrep_blk, packed, residual, n_row, n_col):
    parts, rows, width = packed.shape
    pairs, depth = amp.shape
    return pl.pallas_call(
        functools.partial(ladder_kernel, per_step=width // GRAIN),
        out_shape=jax.ShapeDtypeStruct(residual.shape, jnp.bfloat16),
        grid_spec=pltpu.PrefetchScalarGridSpec(
            num_scalar_prefetch=1,
            grid=(parts,),
            in_specs=[
                pl.BlockSpec((NIRREP, depth), lambda i, s: (0, 0)),
                pl.BlockSpec((pairs, depth), lambda i, s: (0, 0)),
                pl.BlockSpec((1, rows, width), lambda i, s: ((i % n_row) * n_col + i // n_row, 0, 0)),
                pl.BlockSpec((pairs, width), lambda i, s: (0, i)),
            ],
            out_specs=pl.BlockSpec((pairs, width), lambda i, s: (0, i)),
            scratch_shapes=[pltpu.VMEM((NIRREP, pairs, rows), jnp.bfloat16)],
        ),
        compiler_params=pltpu.CompilerParams(vmem_limit_bytes=24 * MIB),
    )(irrep_blk, slot, amp, packed, residual)


def per_device(n_row, n_col, amplitudes, integrals, pair_irrep, block_offset, residual):
    steps, local_k, ab_local = integrals.shape
    n1 = steps * local_k
    cap1 = round_up(-(-n1 // 3), 16)
    cap2 = round_up(-(-n1 * n_row // 6), 16)
    row, col = lax.axis_index("row"), lax.axis_index("col")

    labels = pair_irrep.reshape(steps, n_row, local_k).transpose(1, 0, 2).reshape(n_row, n1)
    irreps = lax.iota(jnp.int32, NIRREP)
    mine = labels[None] == irreps[:, None, None]
    running = jnp.cumsum(mine.astype(jnp.int32), axis=2)
    count = running[:, :, -1]
    rank = jnp.where(mine, running - 1, -1)
    upto = jnp.cumsum(count, axis=1)
    base = upto - count
    fits = (jnp.max(count) <= cap1) & (jnp.max(upto) <= cap2)

    slot1 = lax.dynamic_index_in_dim(rank, row, axis=1, keepdims=False)
    spot = lax.iota(jnp.int32, cap1)
    slot2 = jnp.where(spot[None, None] < count[:, :, None], base[:, :, None] + spot, -1)
    slot2 = slot2.reshape(NIRREP, n_row * cap1)
    slot3 = jnp.where(mine, base[:, :, None] + rank, -1)
    slot3 = slot3.reshape(NIRREP, n_row, steps, local_k).transpose(0, 2, 1, 3).reshape(NIRREP, -1)

    blocks = n_col * ab_local // GRAIN
    starts = lax.iota(jnp.int32, blocks) * GRAIN
    irrep_blk = jnp.sum((starts[:, None] >= block_offset[None, 1:-1]).astype(jnp.int32), axis=1)

    def sparse(amplitudes, integrals, residual):
        per_col = ab_local // GRAIN
        mine1 = pack(integrals, slot1, irrep_blk, col * per_col, cap1, n_row)
        ours = lax.all_to_all(mine1, "row", split_axis=0, concat_axis=0, tiled=True)
        ours = ours.reshape(n_row * cap1, ab_local // n_row)
        first = col * per_col + row * (per_col // n_row)
        mine2 = pack(ours, slot2, irrep_blk, first, cap2, 1)
        packed = lax.all_gather(mine2, ("row", "col"), axis=0, tiled=True)
        amp = amplitudes.reshape(amplitudes.shape[0], -1)
        return ladder_add(amp, slot3, irrep_blk, packed, residual, n_row, n_col)

    def full(amplitudes, integrals, residual):
        return dense(amplitudes, integrals, pair_irrep, block_offset, residual)

    return lax.cond(fits, sparse, full, amplitudes, integrals, residual)


def solution(mesh):
    in_specs = (
        P(("row", "col"), None, None),
        P(None, "row", "col"),
        P(),
        P(),
        P(("row", "col"), None),
    )
    out_specs = P(("row", "col"), None)
    body = functools.partial(per_device, mesh.shape["row"], mesh.shape["col"])
    return jax.shard_map(
        body, mesh=mesh, in_specs=in_specs, out_specs=out_specs, check_vma=False
    )
```

```python
import functools

import jax
import jax.numpy as jnp
from jax import lax
from jax.experimental import pallas as pl
from jax.experimental.pallas import tpu as pltpu
from jax.sharding import PartitionSpec as P

NIRREP = 8
GRAIN = 128
MIB = 1024 * 1024


def apply_piece(irrep_ab, amp_panel, labels, total, piece):
    kept = jnp.where(labels[:, None] == irrep_ab[None, :], piece, jnp.zeros((), piece.dtype))
    return total + jnp.dot(amp_panel, kept, preferred_element_type=jnp.float32)


def dense(amplitudes, integrals, pair_irrep, block_offset, residual):
    ab_local = integrals.shape[2]
    steps = integrals.shape[0]
    position = lax.axis_index("col") * ab_local + lax.iota(jnp.int32, ab_local)
    irrep_ab = jnp.sum((position[:, None] >= block_offset[None, 1:-1]).astype(jnp.int32), axis=1)
    grid_amps = lax.all_to_all(amplitudes, "col", split_axis=2, concat_axis=0, tiled=True)
    panels = [
        lax.all_gather(grid_amps[:, step, :], "col", axis=1, tiled=True) for step in range(steps)
    ]
    total = jnp.zeros((panels[0].shape[0], ab_local), jnp.float32)
    piece = lax.all_gather(integrals, "row", axis=1, tiled=True)
    for step in range(steps):
        total = apply_piece(irrep_ab, panels[step], pair_irrep[step], total, piece[step])
    ladder_half = total.astype(jnp.bfloat16)
    returned = lax.all_to_all(ladder_half, "col", split_axis=0, concat_axis=1, tiled=True)
    return (residual.astype(jnp.float32) + returned.astype(jnp.float32)).astype(jnp.bfloat16)


def round_up(value, grain):
    return (value + grain - 1) // grain * grain


def one_hot_rows(slot_ref, g, rows):
    width = slot_ref.shape[1]
    line = slot_ref[pl.ds(g, 1), :]
    at = lax.broadcasted_iota(jnp.int32, (rows, width), 0)
    return jnp.where(line == at, 1.0, 0.0).astype(jnp.bfloat16)


def pack_kernel(irrep_ref, slot_ref, x_ref, out_ref, pick, *, blocks, per_step):
    rows = pick.shape[1]

    @pl.when(pl.program_id(0) == 0)
    def _():
        for g in range(NIRREP):
            pick[g] = one_hot_rows(slot_ref, g, rows)

    x = x_ref[...].reshape(-1, x_ref.shape[-1])
    first = irrep_ref[blocks] + pl.program_id(0) * per_step
    for t in range(per_step):
        g = irrep_ref[first + t]
        cols = slice(t * GRAIN, (t + 1) * GRAIN)
        packed = jnp.dot(pick[g], x[:, cols], preferred_element_type=jnp.float32)
        out_ref[0, :, cols] = packed.astype(jnp.bfloat16)


def pack(x, slot, irrep_blk, first, rows, parts):
    width = x.shape[-1] // parts
    depth = slot.shape[1]
    blocks = irrep_blk.shape[0]
    scalars = jnp.concatenate([irrep_blk, first[None].astype(jnp.int32)])
    lead = x.ndim - 1
    return pl.pallas_call(
        functools.partial(pack_kernel, blocks=blocks, per_step=width // GRAIN),
        out_shape=jax.ShapeDtypeStruct((parts, rows, width), jnp.bfloat16),
        grid_spec=pltpu.PrefetchScalarGridSpec(
            num_scalar_prefetch=1,
            grid=(parts,),
            in_specs=[
                pl.BlockSpec((NIRREP, depth), lambda i, s: (0, 0)),
                pl.BlockSpec(x.shape[:-1] + (width,), lambda i, s: (0,) * lead + (i,)),
            ],
            out_specs=pl.BlockSpec((1, rows, width), lambda i, s: (i, 0, 0)),
            scratch_shapes=[pltpu.VMEM((NIRREP, rows, depth), jnp.bfloat16)],
        ),
        compiler_params=pltpu.CompilerParams(vmem_limit_bytes=24 * MIB),
    )(scalars, slot, x)


def ladder_kernel(irrep_ref, slot_ref, amp_ref, packed_ref, res_ref, out_ref, amps, *, per_step):
    rows = amps.shape[2]

    @pl.when(pl.program_id(0) == 0)
    def _():
        for g in range(NIRREP):
            pick = one_hot_rows(slot_ref, g, rows)
            amps[g] = lax.dot_general(
                amp_ref[...], pick, (((1,), (1,)), ((), ())), preferred_element_type=jnp.float32
            ).astype(jnp.bfloat16)

    first = pl.program_id(0) * per_step
    for t in range(per_step):
        g = irrep_ref[first + t]
        cols = slice(t * GRAIN, (t + 1) * GRAIN)
        ladder = jnp.dot(amps[g], packed_ref[0, :, cols], preferred_element_type=jnp.float32)
        ladder = ladder.astype(jnp.bfloat16).astype(jnp.float32)
        out_ref[:, cols] = (res_ref[:, cols].astype(jnp.float32) + ladder).astype(jnp.bfloat16)


def ladder_add(amp, slot, irrep_blk, packed, residual, n_row, n_col):
    parts, rows, width = packed.shape
    pairs, depth = amp.shape
    return pl.pallas_call(
        functools.partial(ladder_kernel, per_step=width // GRAIN),
        out_shape=jax.ShapeDtypeStruct(residual.shape, jnp.bfloat16),
        grid_spec=pltpu.PrefetchScalarGridSpec(
            num_scalar_prefetch=1,
            grid=(parts,),
            in_specs=[
                pl.BlockSpec((NIRREP, depth), lambda i, s: (0, 0)),
                pl.BlockSpec((pairs, depth), lambda i, s: (0, 0)),
                pl.BlockSpec((1, rows, width), lambda i, s: ((i % n_row) * n_col + i // n_row, 0, 0)),
                pl.BlockSpec((pairs, width), lambda i, s: (0, i)),
            ],
            out_specs=pl.BlockSpec((pairs, width), lambda i, s: (0, i)),
            scratch_shapes=[pltpu.VMEM((NIRREP, pairs, rows), jnp.bfloat16)],
        ),
        compiler_params=pltpu.CompilerParams(vmem_limit_bytes=24 * MIB),
    )(irrep_blk, slot, amp, packed, residual)


def spread_kernel(
    irrep_ref, slot_ref, amp_ref, mine_ref, res_ref, out_ref, amps, held, sent, got, got_b, *, per_step
):
    n_row, n_col = 8, 4
    row, z = lax.axis_index("row"), lax.axis_index("col")
    rows = amps.shape[2]
    half = round_up(rows // 2, 16)
    top, bottom = pl.ds(0, half), pl.ds(half, rows - half)
    core, x, y = row % 2, (row // 2) % 2, row // 4
    sib = row + 1 - 2 * core
    xn = row + 2 - 4 * x
    yn = row + 4 - 8 * y
    dg = xn + 4 - 8 * y
    far = z // 2
    middle = z + far * (3 - 2 * z)
    order = [middle, 1 - middle, 2, 3]
    order = [o + far * (3 - 2 * o) for o in order]
    inner = z + 1 - 2 * far
    outer = z - 1 + 2 * far

    def place(r, c):
        return {"row": r, "col": c}

    def send(kind, j, r, to, part=None, recv=got):
        slot = r * n_col + order[j]
        ref = held.at[slot] if part is None else held.at[slot, part]
        return pltpu.make_async_remote_copy(
            src_ref=ref,
            dst_ref=ref,
            send_sem=sent.at[kind, j],
            recv_sem=recv.at[slot],
            device_id=to,
            device_id_type=pl.DeviceIdType.MESH,
        )

    def await_chunk(j, r, part=None, recv=got):
        send(0, j, r, place(sib, z), part, recv).wait_recv()

    def compute(j, r_first, r_other):
        def body(i, carry):
            r = r_first + i * (r_other - r_first)
            chunk = order[j] * n_row + r
            slot = r * n_col + order[j]
            for t in range(per_step):
                g = irrep_ref[chunk * per_step + t]
                cols = pl.ds(pl.multiple_of((chunk * per_step + t) * GRAIN, GRAIN), GRAIN)
                piece = held[slot, :, t * GRAIN:(t + 1) * GRAIN]
                ladder = jnp.dot(amps[g], piece, preferred_element_type=jnp.float32)
                ladder = ladder.astype(jnp.bfloat16).astype(jnp.float32)
                total = res_ref[:, cols].astype(jnp.float32) + ladder
                out_ref[:, cols] = total.astype(jnp.bfloat16)
            return carry

        lax.fori_loop(0, 2, body, 0)

    def by_z(j):
        if j == 0:
            return [(send(0, 0, row, place(row, inner)), False), (send(1, 0, row, place(row, outer)), True)]
        to = inner if j == 1 else outer
        return [(send(0 if j == 1 else 1, j, row, place(row, to)), True)]

    def guarded(only_middle, act):
        if only_middle:
            pl.when(middle == 1)(act)
        else:
            act()

    in_plane = lambda j: [
        send(2, j, row, place(xn, z)),
        send(3, j, row, place(yn, z)),
        send(4, j, row, place(sib, z)),
    ]
    from_x = lambda j: [
        send(5, j, xn, place(yn, z), top),
        send(7, j, xn, place(sib, z)),
    ]
    from_y = lambda j: [
        send(6, j, yn, place(xn, z), bottom, got_b),
        send(8, j, yn, place(sib, z)),
    ]
    from_dg = lambda j: [send(9, j, dg, place(sib, z))]

    def own(j):
        if j > 0:
            await_chunk(j, row)
        for copy, only_middle in by_z(j):
            guarded(only_middle, copy.start)
        for copy in in_plane(j):
            copy.start()

    def near(j):
        await_chunk(j, xn)
        for copy in from_x(j):
            copy.start()
        await_chunk(j, yn)
        for copy in from_y(j):
            copy.start()

    def diagonal(j):
        await_chunk(j, dg, top)
        await_chunk(j, dg, bottom, got_b)
        for copy in from_dg(j):
            copy.start()

    def of_core(r):
        return r + 1 - 2 * core

    def own_done(j):
        await_chunk(j, sib)
        compute(j, row, sib)

    def near_done(j):
        await_chunk(j, of_core(xn))
        compute(j, xn, of_core(xn))
        await_chunk(j, of_core(yn))
        compute(j, yn, of_core(yn))

    def diagonal_done(j):
        await_chunk(j, of_core(dg))
        compute(j, dg, of_core(dg))

    barrier = pltpu.get_barrier_semaphore()

    def greet(to):
        pl.semaphore_signal(barrier, inc=1, device_id=to, device_id_type=pl.DeviceIdType.MESH)

    for to in (place(sib, z), place(xn, z), place(yn, z), place(row, inner)):
        greet(to)
    pl.when(middle == 1)(lambda: greet(place(row, outer)))
    held[row * n_col + z] = mine_ref[0]
    pl.semaphore_wait(barrier, 4 + middle)

    own(0)
    for g in range(NIRREP):
        pick = one_hot_rows(slot_ref, g, rows)
        amps[g] = lax.dot_general(
            amp_ref[...], pick, (((1,), (1,)), ((), ())), preferred_element_type=jnp.float32
        ).astype(jnp.bfloat16)
    own_done(0)
    own(1)
    near(0)
    own_done(1)
    near_done(0)
    own(2)
    near(1)
    diagonal(0)
    own_done(2)
    near_done(1)
    diagonal_done(0)
    own(3)
    near(2)
    diagonal(1)
    own_done(3)
    near_done(2)
    diagonal_done(1)
    near(3)
    diagonal(2)
    near_done(3)
    diagonal_done(2)
    diagonal(3)
    diagonal_done(3)

    for j in range(n_col):
        for copy, only_middle in by_z(j):
            guarded(only_middle, copy.wait_send)
        for copy in in_plane(j) + from_x(j) + from_y(j) + from_dg(j):
            copy.wait_send()


def spread_add(amp, slot, irrep_blk, mine, residual, n_row, n_col):
    _, rows, width = mine.shape
    parts = n_row * n_col
    vmem = pl.BlockSpec(memory_space=pltpu.VMEM)
    return pl.pallas_call(
        functools.partial(spread_kernel, per_step=width // GRAIN),
        out_shape=jax.ShapeDtypeStruct(residual.shape, jnp.bfloat16),
        in_specs=[pl.BlockSpec(memory_space=pltpu.SMEM), vmem, vmem, vmem, vmem],
        out_specs=vmem,
        scratch_shapes=[
            pltpu.VMEM((NIRREP, amp.shape[0], rows), jnp.bfloat16),
            pltpu.VMEM((parts, rows, width), jnp.bfloat16),
            pltpu.SemaphoreType.DMA((10, n_col)),
            pltpu.SemaphoreType.DMA((parts,)),
            pltpu.SemaphoreType.DMA((parts,)),
        ],
        compiler_params=pltpu.CompilerParams(
            vmem_limit_bytes=48 * MIB, collective_id=0, has_side_effects=True
        ),
    )(irrep_blk, slot, amp, mine, residual)


def per_device(n_row, n_col, amplitudes, integrals, pair_irrep, block_offset, residual):
    steps, local_k, ab_local = integrals.shape
    n1 = steps * local_k
    cap1 = round_up(-(-n1 // 3), 16)
    cap2 = round_up(-(-n1 * n_row // 6), 16)
    row, col = lax.axis_index("row"), lax.axis_index("col")

    labels = pair_irrep.reshape(steps, n_row, local_k).transpose(1, 0, 2).reshape(n_row, n1)
    irreps = lax.iota(jnp.int32, NIRREP)
    mine = labels[None] == irreps[:, None, None]
    running = jnp.cumsum(mine.astype(jnp.int32), axis=2)
    count = running[:, :, -1]
    rank = jnp.where(mine, running - 1, -1)
    upto = jnp.cumsum(count, axis=1)
    base = upto - count
    fits = (jnp.max(count) <= cap1) & (jnp.max(upto) <= cap2)

    slot1 = lax.dynamic_index_in_dim(rank, row, axis=1, keepdims=False)
    spot = lax.iota(jnp.int32, cap1)
    slot2 = jnp.where(spot[None, None] < count[:, :, None], base[:, :, None] + spot, -1)
    slot2 = slot2.reshape(NIRREP, n_row * cap1)
    slot3 = jnp.where(mine, base[:, :, None] + rank, -1)
    slot3 = slot3.reshape(NIRREP, n_row, steps, local_k).transpose(0, 2, 1, 3).reshape(NIRREP, -1)

    blocks = n_col * ab_local // GRAIN
    starts = lax.iota(jnp.int32, blocks) * GRAIN
    irrep_blk = jnp.sum((starts[:, None] >= block_offset[None, 1:-1]).astype(jnp.int32), axis=1)

    def sparse(amplitudes, integrals, residual):
        per_col = ab_local // GRAIN
        mine1 = pack(integrals, slot1, irrep_blk, col * per_col, cap1, n_row)
        ours = lax.all_to_all(mine1, "row", split_axis=0, concat_axis=0, tiled=True)
        ours = ours.reshape(n_row * cap1, ab_local // n_row)
        first = col * per_col + row * (per_col // n_row)
        mine2 = pack(ours, slot2, irrep_blk, first, cap2, 1)
        amp = amplitudes.reshape(amplitudes.shape[0], -1)
        if (n_row, n_col) == (8, 4):
            return spread_add(amp, slot3, irrep_blk, mine2, residual, n_row, n_col)
        packed = lax.all_gather(mine2, ("row", "col"), axis=0, tiled=True)
        return ladder_add(amp, slot3, irrep_blk, packed, residual, n_row, n_col)

    def full(amplitudes, integrals, residual):
        return dense(amplitudes, integrals, pair_irrep, block_offset, residual)

    return lax.cond(fits, sparse, full, amplitudes, integrals, residual)


def solution(mesh):
    in_specs = (
        P(("row", "col"), None, None),
        P(None, "row", "col"),
        P(),
        P(),
        P(("row", "col"), None),
    )
    out_specs = P(("row", "col"), None)
    body = functools.partial(per_device, mesh.shape["row"], mesh.shape["col"])
    return jax.shard_map(
        body, mesh=mesh, in_specs=in_specs, out_specs=out_specs, check_vma=False
    )
```

```python
import functools

import jax
import jax.numpy as jnp
from jax import lax
from jax.experimental import pallas as pl
from jax.experimental.pallas import tpu as pltpu
from jax.sharding import PartitionSpec as P

NIRREP = 8
GRAIN = 128
MIB = 1024 * 1024


def apply_piece(irrep_ab, amp_panel, labels, total, piece):
    kept = jnp.where(labels[:, None] == irrep_ab[None, :], piece, jnp.zeros((), piece.dtype))
    return total + jnp.dot(amp_panel, kept, preferred_element_type=jnp.float32)


def dense(amplitudes, integrals, pair_irrep, block_offset, residual):
    ab_local = integrals.shape[2]
    steps = integrals.shape[0]
    position = lax.axis_index("col") * ab_local + lax.iota(jnp.int32, ab_local)
    irrep_ab = jnp.sum((position[:, None] >= block_offset[None, 1:-1]).astype(jnp.int32), axis=1)
    grid_amps = lax.all_to_all(amplitudes, "col", split_axis=2, concat_axis=0, tiled=True)
    panels = [
        lax.all_gather(grid_amps[:, step, :], "col", axis=1, tiled=True) for step in range(steps)
    ]
    total = jnp.zeros((panels[0].shape[0], ab_local), jnp.float32)
    piece = lax.all_gather(integrals, "row", axis=1, tiled=True)
    for step in range(steps):
        total = apply_piece(irrep_ab, panels[step], pair_irrep[step], total, piece[step])
    ladder_half = total.astype(jnp.bfloat16)
    returned = lax.all_to_all(ladder_half, "col", split_axis=0, concat_axis=1, tiled=True)
    return (residual.astype(jnp.float32) + returned.astype(jnp.float32)).astype(jnp.bfloat16)


def round_up(value, grain):
    return (value + grain - 1) // grain * grain


def one_hot_rows(slot_ref, g, rows):
    width = slot_ref.shape[1]
    line = slot_ref[pl.ds(g, 1), :]
    at = lax.broadcasted_iota(jnp.int32, (rows, width), 0)
    return jnp.where(line == at, 1.0, 0.0).astype(jnp.bfloat16)


def pack_kernel(irrep_ref, slot_ref, x_ref, out_ref, pick, *, blocks, per_step):
    rows = pick.shape[1]

    @pl.when(pl.program_id(0) == 0)
    def _():
        for g in range(NIRREP):
            pick[g] = one_hot_rows(slot_ref, g, rows)

    x = x_ref[...].reshape(-1, x_ref.shape[-1])
    first = irrep_ref[blocks] + pl.program_id(0) * per_step
    for t in range(per_step):
        g = irrep_ref[first + t]
        cols = slice(t * GRAIN, (t + 1) * GRAIN)
        packed = jnp.dot(pick[g], x[:, cols], preferred_element_type=jnp.float32)
        out_ref[0, :, cols] = packed.astype(jnp.bfloat16)


def pack(x, slot, irrep_blk, first, rows, parts):
    width = x.shape[-1] // parts
    depth = slot.shape[1]
    blocks = irrep_blk.shape[0]
    scalars = jnp.concatenate([irrep_blk, first[None].astype(jnp.int32)])
    lead = x.ndim - 1
    return pl.pallas_call(
        functools.partial(pack_kernel, blocks=blocks, per_step=width // GRAIN),
        out_shape=jax.ShapeDtypeStruct((parts, rows, width), jnp.bfloat16),
        grid_spec=pltpu.PrefetchScalarGridSpec(
            num_scalar_prefetch=1,
            grid=(parts,),
            in_specs=[
                pl.BlockSpec((NIRREP, depth), lambda i, s: (0, 0)),
                pl.BlockSpec(x.shape[:-1] + (width,), lambda i, s: (0,) * lead + (i,)),
            ],
            out_specs=pl.BlockSpec((1, rows, width), lambda i, s: (i, 0, 0)),
            scratch_shapes=[pltpu.VMEM((NIRREP, rows, depth), jnp.bfloat16)],
        ),
        compiler_params=pltpu.CompilerParams(vmem_limit_bytes=24 * MIB),
    )(scalars, slot, x)


def ladder_kernel(irrep_ref, slot_ref, amp_ref, packed_ref, res_ref, out_ref, amps, *, per_step):
    rows = amps.shape[2]

    @pl.when(pl.program_id(0) == 0)
    def _():
        for g in range(NIRREP):
            pick = one_hot_rows(slot_ref, g, rows)
            amps[g] = lax.dot_general(
                amp_ref[...], pick, (((1,), (1,)), ((), ())), preferred_element_type=jnp.float32
            ).astype(jnp.bfloat16)

    first = pl.program_id(0) * per_step
    for t in range(per_step):
        g = irrep_ref[first + t]
        cols = slice(t * GRAIN, (t + 1) * GRAIN)
        ladder = jnp.dot(amps[g], packed_ref[0, :, cols], preferred_element_type=jnp.float32)
        ladder = ladder.astype(jnp.bfloat16).astype(jnp.float32)
        out_ref[:, cols] = (res_ref[:, cols].astype(jnp.float32) + ladder).astype(jnp.bfloat16)


def ladder_add(amp, slot, irrep_blk, packed, residual, n_row, n_col):
    parts, rows, width = packed.shape
    pairs, depth = amp.shape
    return pl.pallas_call(
        functools.partial(ladder_kernel, per_step=width // GRAIN),
        out_shape=jax.ShapeDtypeStruct(residual.shape, jnp.bfloat16),
        grid_spec=pltpu.PrefetchScalarGridSpec(
            num_scalar_prefetch=1,
            grid=(parts,),
            in_specs=[
                pl.BlockSpec((NIRREP, depth), lambda i, s: (0, 0)),
                pl.BlockSpec((pairs, depth), lambda i, s: (0, 0)),
                pl.BlockSpec((1, rows, width), lambda i, s: ((i % n_row) * n_col + i // n_row, 0, 0)),
                pl.BlockSpec((pairs, width), lambda i, s: (0, i)),
            ],
            out_specs=pl.BlockSpec((pairs, width), lambda i, s: (0, i)),
            scratch_shapes=[pltpu.VMEM((NIRREP, pairs, rows), jnp.bfloat16)],
        ),
        compiler_params=pltpu.CompilerParams(vmem_limit_bytes=24 * MIB),
    )(irrep_blk, slot, amp, packed, residual)


def spread_kernel(
    irrep_ref, slot_ref, amp_ref, mine_ref, res_ref, out_ref, amps, held, sent, got, got_b, got_c, *, per_step
):
    n_row, n_col = 8, 4
    row, z = lax.axis_index("row"), lax.axis_index("col")
    rows = amps.shape[2]
    half = round_up(rows // 2, 16)
    along_rows = rows - 32
    along_part = pl.ds(0, along_rows)

    def top(j):
        return pl.ds(0, half) if j == 0 else pl.ds(along_rows, 16)

    def bottom(j):
        return pl.ds(half, rows - half) if j == 0 else pl.ds(along_rows + 16, 16)

    core, x, y = row % 2, (row // 2) % 2, row // 4
    sib = row + 1 - 2 * core
    xn = row + 2 - 4 * x
    yn = row + 4 - 8 * y
    dg = xn + 4 - 8 * y
    far = z // 2
    middle = z + far * (3 - 2 * z)
    order = [middle, 1 - middle, 2, 3]
    order = [o + far * (3 - 2 * o) for o in order]
    inner = z + 1 - 2 * far
    outer = z - 1 + 2 * far

    def place(r, c):
        return {"row": r, "col": c}

    def send(kind, j, r, to, part=None, recv=got):
        slot = r * n_col + order[j]
        ref = held.at[slot] if part is None else held.at[slot, part]
        return pltpu.make_async_remote_copy(
            src_ref=ref,
            dst_ref=ref,
            send_sem=sent.at[kind, j],
            recv_sem=recv.at[slot],
            device_id=to,
            device_id_type=pl.DeviceIdType.MESH,
        )

    def await_chunk(j, r, part=None, recv=got):
        send(0, j, r, place(sib, z), part, recv).wait_recv()

    def compute(j, r_first, r_other):
        def body(i, carry):
            r = r_first + i * (r_other - r_first)
            chunk = order[j] * n_row + r
            slot = r * n_col + order[j]
            for t in range(per_step):
                g = irrep_ref[chunk * per_step + t]
                cols = pl.ds(pl.multiple_of((chunk * per_step + t) * GRAIN, GRAIN), GRAIN)
                piece = held[slot, :, t * GRAIN:(t + 1) * GRAIN]
                ladder = jnp.dot(amps[g], piece, preferred_element_type=jnp.float32)
                ladder = ladder.astype(jnp.bfloat16).astype(jnp.float32)
                total = res_ref[:, cols].astype(jnp.float32) + ladder
                out_ref[:, cols] = total.astype(jnp.bfloat16)
            return carry

        lax.fori_loop(0, 2, body, 0)

    def by_z(j, r=row, part=None, recv=got, kind=0):
        if j == 0:
            return [
                (send(kind, 0, r, place(row, inner), part, recv), False),
                (send(kind + 1, 0, r, place(row, outer), part, recv), True),
            ]
        to = inner if j == 1 else outer
        return [(send(kind if j == 1 else kind + 1, j, r, place(row, to), part, recv), True)]

    def dg_by_z(j):
        return by_z(j, dg, along_part, got_c, 10)

    def guarded(only_middle, act):
        if only_middle:
            pl.when(middle == 1)(act)
        else:
            act()

    in_plane = lambda j: [
        send(2, j, row, place(xn, z)),
        send(3, j, row, place(yn, z)),
        send(4, j, row, place(sib, z)),
    ]
    from_x = lambda j: [
        send(5, j, xn, place(yn, z), top(j)),
        send(7, j, xn, place(sib, z)),
    ]
    from_y = lambda j: [
        send(6, j, yn, place(xn, z), bottom(j), got_b),
        send(8, j, yn, place(sib, z)),
    ]
    from_dg = lambda j: [send(9, j, dg, place(sib, z))]

    def own(j):
        if j > 0:
            await_chunk(j, row)
        for copy, only_middle in by_z(j):
            guarded(only_middle, copy.start)
        for copy in in_plane(j):
            copy.start()

    def near(j):
        await_chunk(j, xn)
        for copy in from_x(j):
            copy.start()
        await_chunk(j, yn)
        for copy in from_y(j):
            copy.start()

    def along(j):
        await_chunk(j, dg, along_part, got_c)
        for copy, only_middle in dg_by_z(j):
            guarded(only_middle, copy.start)

    def diagonal(j):
        await_chunk(j, dg, top(j))
        await_chunk(j, dg, bottom(j), got_b)
        if j == 0:
            for copy, only_middle in dg_by_z(0):
                guarded(only_middle, copy.start)
        for copy in from_dg(j):
            copy.start()

    def of_core(r):
        return r + 1 - 2 * core

    def own_done(j):
        await_chunk(j, sib)
        compute(j, row, sib)

    def near_done(j):
        await_chunk(j, of_core(xn))
        compute(j, xn, of_core(xn))
        await_chunk(j, of_core(yn))
        compute(j, yn, of_core(yn))

    def diagonal_done(j):
        await_chunk(j, of_core(dg))
        compute(j, dg, of_core(dg))

    barrier = pltpu.get_barrier_semaphore()

    def greet(to):
        pl.semaphore_signal(barrier, inc=1, device_id=to, device_id_type=pl.DeviceIdType.MESH)

    for to in (place(sib, z), place(xn, z), place(yn, z), place(row, inner)):
        greet(to)
    pl.when(middle == 1)(lambda: greet(place(row, outer)))
    held[row * n_col + z] = mine_ref[0]
    pl.semaphore_wait(barrier, 4 + middle)

    own(0)
    for g in range(NIRREP):
        pick = one_hot_rows(slot_ref, g, rows)
        amps[g] = lax.dot_general(
            amp_ref[...], pick, (((1,), (1,)), ((), ())), preferred_element_type=jnp.float32
        ).astype(jnp.bfloat16)
    own_done(0)
    own(1)
    near(0)
    own_done(1)
    own(2)
    near(1)
    near_done(0)
    diagonal(0)
    own(3)
    own_done(2)
    near_done(1)
    along(1)
    near(2)
    diagonal_done(0)
    own_done(3)
    along(2)
    diagonal(1)
    near_done(2)
    near(3)
    along(3)
    diagonal(2)
    diagonal_done(1)
    diagonal(3)
    near_done(3)
    diagonal_done(2)
    diagonal_done(3)

    for j in range(n_col):
        for copy, only_middle in by_z(j) + dg_by_z(j):
            guarded(only_middle, copy.wait_send)
        for copy in in_plane(j) + from_x(j) + from_y(j) + from_dg(j):
            copy.wait_send()


def spread_add(amp, slot, irrep_blk, mine, residual, n_row, n_col):
    _, rows, width = mine.shape
    parts = n_row * n_col
    vmem = pl.BlockSpec(memory_space=pltpu.VMEM)
    return pl.pallas_call(
        functools.partial(spread_kernel, per_step=width // GRAIN),
        out_shape=jax.ShapeDtypeStruct(residual.shape, jnp.bfloat16),
        in_specs=[pl.BlockSpec(memory_space=pltpu.SMEM), vmem, vmem, vmem, vmem],
        out_specs=vmem,
        scratch_shapes=[
            pltpu.VMEM((NIRREP, amp.shape[0], rows), jnp.bfloat16),
            pltpu.VMEM((parts, rows, width), jnp.bfloat16),
            pltpu.SemaphoreType.DMA((12, n_col)),
            pltpu.SemaphoreType.DMA((parts,)),
            pltpu.SemaphoreType.DMA((parts,)),
            pltpu.SemaphoreType.DMA((parts,)),
        ],
        compiler_params=pltpu.CompilerParams(
            vmem_limit_bytes=48 * MIB, collective_id=0, has_side_effects=True
        ),
    )(irrep_blk, slot, amp, mine, residual)


def exchange_kernel(
    irrep_ref, slot1_ref, slot2_ref, x_ref, out_ref,
    x, mine, ours, pick1, pick2, loaded, sent, got, *, n_row, per_step
):
    row, col = lax.axis_index("row"), lax.axis_index("col")
    width = per_step * GRAIN
    cap1, cap2 = pick1.shape[1], pick2.shape[1]
    turns = list(range(1, n_row)) + [0]

    def peer(k):
        return (row + k) % n_row

    def load(k):
        cols = pl.ds(pl.multiple_of(peer(k) * width, width), width)
        return pltpu.make_async_copy(x_ref.at[:, :, cols], x.at[k], loaded.at[k])

    def send(k):
        return pltpu.make_async_remote_copy(
            src_ref=mine.at[k],
            dst_ref=ours.at[row],
            send_sem=sent.at[k],
            recv_sem=got.at[row],
            device_id={"row": peer(k), "col": col},
            device_id_type=pl.DeviceIdType.MESH,
        )

    for k in turns:
        load(k).start()
    barrier = pltpu.get_barrier_semaphore()
    for k in turns[:-1]:
        pl.semaphore_signal(
            barrier, inc=1, device_id={"row": peer(k), "col": col},
            device_id_type=pl.DeviceIdType.MESH,
        )
    for g in range(NIRREP):
        pick1[g] = one_hot_rows(slot1_ref, g, cap1)

    def pack_into(put, picks, rows, block, first):
        for t in range(0, per_step, 2):
            two = jnp.concatenate([picks[irrep_ref[first + t]], picks[irrep_ref[first + t + 1]]], axis=0)
            both = jnp.dot(
                two, block[:, t * GRAIN:(t + 2) * GRAIN], preferred_element_type=jnp.float32
            ).astype(jnp.bfloat16)
            put(t, both[:rows, :GRAIN])
            put(t + 1, both[rows:, GRAIN:])

    for k in turns:
        load(k).wait()
        block = x[k].reshape(-1, width)
        first = (col * n_row + peer(k)) * per_step

        def put(t, piece):
            cols = slice(t * GRAIN, (t + 1) * GRAIN)
            if k > 0:
                mine[k, :, cols] = piece
            else:
                ours[row, :, cols] = piece

        pack_into(put, pick1, cap1, block, first)
        if k == turns[0]:
            pl.semaphore_wait(barrier, n_row - 1)
        if k > 0:
            send(k).start()

    for g in range(NIRREP):
        pick2[g] = one_hot_rows(slot2_ref, g, cap2)
    for k in turns[:-1]:
        source = (row + n_row - k) % n_row
        pltpu.make_async_copy(mine.at[k], ours.at[source], got.at[source]).wait()

    def put_out(t, piece):
        out_ref[0, :, t * GRAIN:(t + 1) * GRAIN] = piece

    block = ours[...].reshape(n_row * cap1, width)
    pack_into(put_out, pick2, cap2, block, (col * n_row + row) * per_step)
    for k in turns[:-1]:
        send(k).wait_send()


def exchange(integrals, slot1, slot2, irrep_blk, cap1, cap2, n_row):
    steps, local_k, ab_local = integrals.shape
    width = ab_local // n_row
    vmem = pl.BlockSpec(memory_space=pltpu.VMEM)
    return pl.pallas_call(
        functools.partial(exchange_kernel, n_row=n_row, per_step=width // GRAIN),
        out_shape=jax.ShapeDtypeStruct((1, cap2, width), jnp.bfloat16),
        in_specs=[pl.BlockSpec(memory_space=pltpu.SMEM), vmem, vmem, pl.BlockSpec(memory_space=pl.ANY)],
        out_specs=vmem,
        scratch_shapes=[
            pltpu.VMEM((n_row, steps, local_k, width), jnp.bfloat16),
            pltpu.VMEM((n_row, cap1, width), jnp.bfloat16),
            pltpu.VMEM((n_row, cap1, width), jnp.bfloat16),
            pltpu.VMEM((NIRREP, cap1, steps * local_k), jnp.bfloat16),
            pltpu.VMEM((NIRREP, cap2, n_row * cap1), jnp.bfloat16),
            pltpu.SemaphoreType.DMA((n_row,)),
            pltpu.SemaphoreType.DMA((n_row,)),
            pltpu.SemaphoreType.DMA((n_row,)),
        ],
        compiler_params=pltpu.CompilerParams(
            vmem_limit_bytes=24 * MIB, collective_id=1, has_side_effects=True
        ),
    )(irrep_blk, slot1, slot2, integrals)


def per_device(n_row, n_col, amplitudes, integrals, pair_irrep, block_offset, residual):
    steps, local_k, ab_local = integrals.shape
    n1 = steps * local_k
    cap1 = round_up(-(-n1 // 3), 16)
    cap2 = round_up(-(-n1 * n_row // 6), 16)
    tight = cap2 - 16
    row, col = lax.axis_index("row"), lax.axis_index("col")

    labels = pair_irrep.reshape(steps, n_row, local_k).transpose(1, 0, 2).reshape(n_row, n1)
    irreps = lax.iota(jnp.int32, NIRREP)
    mine = labels[None] == irreps[:, None, None]
    running = jnp.cumsum(mine.astype(jnp.int32), axis=2)
    count = running[:, :, -1]
    rank = jnp.where(mine, running - 1, -1)
    upto = jnp.cumsum(count, axis=1)
    base = upto - count
    most = jnp.max(upto)
    level = jnp.where(
        jnp.max(count) > cap1, 2, (most > tight).astype(jnp.int32) + (most > cap2).astype(jnp.int32)
    )

    slot1 = lax.dynamic_index_in_dim(rank, row, axis=1, keepdims=False)
    spot = lax.iota(jnp.int32, cap1)
    slot2 = jnp.where(spot[None, None] < count[:, :, None], base[:, :, None] + spot, -1)
    slot2 = slot2.reshape(NIRREP, n_row * cap1)
    slot3 = jnp.where(mine, base[:, :, None] + rank, -1)
    slot3 = slot3.reshape(NIRREP, n_row, steps, local_k).transpose(0, 2, 1, 3).reshape(NIRREP, -1)

    blocks = n_col * ab_local // GRAIN
    starts = lax.iota(jnp.int32, blocks) * GRAIN
    irrep_blk = jnp.sum((starts[:, None] >= block_offset[None, 1:-1]).astype(jnp.int32), axis=1)

    per_col = ab_local // GRAIN

    def by_links(amplitudes, integrals, residual):
        mine = exchange(integrals, slot1, slot2, irrep_blk, cap1, tight, n_row)
        amp = amplitudes.reshape(amplitudes.shape[0], -1)
        return spread_add(amp, slot3, irrep_blk, mine, residual, n_row, n_col)

    def sparse(amplitudes, integrals, residual):
        mine1 = pack(integrals, slot1, irrep_blk, col * per_col, cap1, n_row)
        ours = lax.all_to_all(mine1, "row", split_axis=0, concat_axis=0, tiled=True)
        ours = ours.reshape(n_row * cap1, ab_local // n_row)
        first = col * per_col + row * (per_col // n_row)
        mine2 = pack(ours, slot2, irrep_blk, first, cap2, 1)
        packed = lax.all_gather(mine2, ("row", "col"), axis=0, tiled=True)
        amp = amplitudes.reshape(amplitudes.shape[0], -1)
        return ladder_add(amp, slot3, irrep_blk, packed, residual, n_row, n_col)

    def full(amplitudes, integrals, residual):
        return dense(amplitudes, integrals, pair_irrep, block_offset, residual)

    quick = by_links if (n_row, n_col) == (8, 4) else sparse
    return lax.switch(level, [quick, sparse, full], amplitudes, integrals, residual)


def solution(mesh):
    in_specs = (
        P(("row", "col"), None, None),
        P(None, "row", "col"),
        P(),
        P(),
        P(("row", "col"), None),
    )
    out_specs = P(("row", "col"), None)
    body = functools.partial(per_device, mesh.shape["row"], mesh.shape["col"])
    return jax.shard_map(
        body, mesh=mesh, in_specs=in_specs, out_specs=out_specs, check_vma=False
    )
```

```python
import functools

import jax
import jax.numpy as jnp
import numpy as np
from jax import lax
from jax.experimental import pallas as pl
from jax.experimental.pallas import tpu as pltpu
from jax.sharding import PartitionSpec as P

NIRREP = 8
GRAIN = 128
MIB = 1024 * 1024


def apply_piece(irrep_ab, amp_panel, labels, total, piece):
    kept = jnp.where(labels[:, None] == irrep_ab[None, :], piece, jnp.zeros((), piece.dtype))
    return total + jnp.dot(amp_panel, kept, preferred_element_type=jnp.float32)


def dense(amplitudes, integrals, pair_irrep, block_offset, residual):
    ab_local = integrals.shape[2]
    steps = integrals.shape[0]
    position = lax.axis_index("col") * ab_local + lax.iota(jnp.int32, ab_local)
    irrep_ab = jnp.sum((position[:, None] >= block_offset[None, 1:-1]).astype(jnp.int32), axis=1)
    grid_amps = lax.all_to_all(amplitudes, "col", split_axis=2, concat_axis=0, tiled=True)
    panels = [
        lax.all_gather(grid_amps[:, step, :], "col", axis=1, tiled=True) for step in range(steps)
    ]
    total = jnp.zeros((panels[0].shape[0], ab_local), jnp.float32)
    piece = lax.all_gather(integrals, "row", axis=1, tiled=True)
    for step in range(steps):
        total = apply_piece(irrep_ab, panels[step], pair_irrep[step], total, piece[step])
    ladder_half = total.astype(jnp.bfloat16)
    returned = lax.all_to_all(ladder_half, "col", split_axis=0, concat_axis=1, tiled=True)
    return (residual.astype(jnp.float32) + returned.astype(jnp.float32)).astype(jnp.bfloat16)


def round_up(value, grain):
    return (value + grain - 1) // grain * grain


def one_hot_rows(slot_ref, g, rows):
    width = slot_ref.shape[1]
    line = slot_ref[pl.ds(g, 1), :]
    at = lax.broadcasted_iota(jnp.int32, (rows, width), 0)
    return jnp.where(line == at, 1.0, 0.0).astype(jnp.bfloat16)


def pack_kernel(irrep_ref, slot_ref, x_ref, out_ref, pick, *, blocks, per_step):
    rows = pick.shape[1]

    @pl.when(pl.program_id(0) == 0)
    def _():
        for g in range(NIRREP):
            pick[g] = one_hot_rows(slot_ref, g, rows)

    x = x_ref[...].reshape(-1, x_ref.shape[-1])
    first = irrep_ref[blocks] + pl.program_id(0) * per_step
    for t in range(per_step):
        g = irrep_ref[first + t]
        cols = slice(t * GRAIN, (t + 1) * GRAIN)
        packed = jnp.dot(pick[g], x[:, cols], preferred_element_type=jnp.float32)
        out_ref[0, :, cols] = packed.astype(jnp.bfloat16)


def pack(x, slot, irrep_blk, first, rows, parts):
    width = x.shape[-1] // parts
    depth = slot.shape[1]
    blocks = irrep_blk.shape[0]
    scalars = jnp.concatenate([irrep_blk, first[None].astype(jnp.int32)])
    lead = x.ndim - 1
    return pl.pallas_call(
        functools.partial(pack_kernel, blocks=blocks, per_step=width // GRAIN),
        out_shape=jax.ShapeDtypeStruct((parts, rows, width), jnp.bfloat16),
        grid_spec=pltpu.PrefetchScalarGridSpec(
            num_scalar_prefetch=1,
            grid=(parts,),
            in_specs=[
                pl.BlockSpec((NIRREP, depth), lambda i, s: (0, 0)),
                pl.BlockSpec(x.shape[:-1] + (width,), lambda i, s: (0,) * lead + (i,)),
            ],
            out_specs=pl.BlockSpec((1, rows, width), lambda i, s: (i, 0, 0)),
            scratch_shapes=[pltpu.VMEM((NIRREP, rows, depth), jnp.bfloat16)],
        ),
        compiler_params=pltpu.CompilerParams(vmem_limit_bytes=24 * MIB),
    )(scalars, slot, x)


def ladder_kernel(irrep_ref, slot_ref, amp_ref, packed_ref, res_ref, out_ref, amps, *, per_step):
    rows = amps.shape[2]

    @pl.when(pl.program_id(0) == 0)
    def _():
        for g in range(NIRREP):
            pick = one_hot_rows(slot_ref, g, rows)
            amps[g] = lax.dot_general(
                amp_ref[...], pick, (((1,), (1,)), ((), ())), preferred_element_type=jnp.float32
            ).astype(jnp.bfloat16)

    first = pl.program_id(0) * per_step
    for t in range(per_step):
        g = irrep_ref[first + t]
        cols = slice(t * GRAIN, (t + 1) * GRAIN)
        ladder = jnp.dot(amps[g], packed_ref[0, :, cols], preferred_element_type=jnp.float32)
        ladder = ladder.astype(jnp.bfloat16).astype(jnp.float32)
        out_ref[:, cols] = (res_ref[:, cols].astype(jnp.float32) + ladder).astype(jnp.bfloat16)


def ladder_add(amp, slot, irrep_blk, packed, residual, n_row, n_col):
    parts, rows, width = packed.shape
    pairs, depth = amp.shape
    return pl.pallas_call(
        functools.partial(ladder_kernel, per_step=width // GRAIN),
        out_shape=jax.ShapeDtypeStruct(residual.shape, jnp.bfloat16),
        grid_spec=pltpu.PrefetchScalarGridSpec(
            num_scalar_prefetch=1,
            grid=(parts,),
            in_specs=[
                pl.BlockSpec((NIRREP, depth), lambda i, s: (0, 0)),
                pl.BlockSpec((pairs, depth), lambda i, s: (0, 0)),
                pl.BlockSpec((1, rows, width), lambda i, s: ((i % n_row) * n_col + i // n_row, 0, 0)),
                pl.BlockSpec((pairs, width), lambda i, s: (0, i)),
            ],
            out_specs=pl.BlockSpec((pairs, width), lambda i, s: (0, i)),
            scratch_shapes=[pltpu.VMEM((NIRREP, pairs, rows), jnp.bfloat16)],
        ),
        compiler_params=pltpu.CompilerParams(vmem_limit_bytes=24 * MIB),
    )(irrep_blk, slot, amp, packed, residual)


def spread_kernel(
    irrep_ref, slot_ref, amp_ref, mine_ref, res_hbm, out_hbm,
    amps, held, res_ref, out_ref, sent, got, got_b, got_c, read, wrote, *, per_step
):
    n_row, n_col = 8, 4
    row, z = lax.axis_index("row"), lax.axis_index("col")
    rows = amps.shape[2]
    half = round_up(rows // 2, 16)
    along_rows = rows - 32
    along_part = pl.ds(0, along_rows)

    def top(j):
        return pl.ds(0, half) if j == 0 else pl.ds(along_rows, 16)

    def bottom(j):
        return pl.ds(half, rows - half) if j == 0 else pl.ds(along_rows + 16, 16)

    core, x, y = row % 2, (row // 2) % 2, row // 4
    sib = row + 1 - 2 * core
    xn = row + 2 - 4 * x
    yn = row + 4 - 8 * y
    dg = xn + 4 - 8 * y
    far = z // 2
    middle = z + far * (3 - 2 * z)
    order = [middle, 1 - middle, 2, 3]
    order = [o + far * (3 - 2 * o) for o in order]
    inner = z + 1 - 2 * far
    outer = z - 1 + 2 * far

    def place(r, c):
        return {"row": r, "col": c}

    def send(kind, j, r, to, part=None, recv=got):
        slot = r * n_col + order[j]
        ref = held.at[slot] if part is None else held.at[slot, part]
        return pltpu.make_async_remote_copy(
            src_ref=ref,
            dst_ref=ref,
            send_sem=sent.at[kind, j],
            recv_sem=recv.at[slot],
            device_id=to,
            device_id_type=pl.DeviceIdType.MESH,
        )

    def await_chunk(j, r, part=None, recv=got):
        send(0, j, r, place(sib, z), part, recv).wait_recv()

    def write(r, c):
        width = per_step * GRAIN
        cols = pl.ds(pl.multiple_of((c * n_row + r) * width, width), width)
        return pltpu.make_async_copy(out_ref.at[:, cols], out_hbm.at[:, cols], wrote.at[r * n_col + c])

    def compute(j, r_first, r_other):
        def body(i, carry):
            r = r_first + i * (r_other - r_first)
            chunk = order[j] * n_row + r
            slot = r * n_col + order[j]
            for t in range(per_step):
                g = irrep_ref[chunk * per_step + t]
                cols = pl.ds(pl.multiple_of((chunk * per_step + t) * GRAIN, GRAIN), GRAIN)
                piece = held[slot, :, t * GRAIN:(t + 1) * GRAIN]
                ladder = jnp.dot(amps[g], piece, preferred_element_type=jnp.float32)
                ladder = ladder.astype(jnp.bfloat16).astype(jnp.float32)
                total = res_ref[:, cols].astype(jnp.float32) + ladder
                out_ref[:, cols] = total.astype(jnp.bfloat16)
            write(r, order[j]).start()
            return carry

        lax.fori_loop(0, 2, body, 0)

    def by_z(j, r=row, part=None, recv=got, kind=0):
        if j == 0:
            return [
                (send(kind, 0, r, place(row, inner), part, recv), False),
                (send(kind + 1, 0, r, place(row, outer), part, recv), True),
            ]
        to = inner if j == 1 else outer
        return [(send(kind if j == 1 else kind + 1, j, r, place(row, to), part, recv), True)]

    def dg_by_z(j):
        return by_z(j, dg, along_part, got_c, 10)

    def guarded(only_middle, act):
        if only_middle:
            pl.when(middle == 1)(act)
        else:
            act()

    in_plane = lambda j: [
        send(2, j, row, place(xn, z)),
        send(3, j, row, place(yn, z)),
        send(4, j, row, place(sib, z)),
    ]
    from_x = lambda j: [
        send(5, j, xn, place(yn, z), top(j)),
        send(7, j, xn, place(sib, z)),
    ]
    from_y = lambda j: [
        send(6, j, yn, place(xn, z), bottom(j), got_b),
        send(8, j, yn, place(sib, z)),
    ]
    from_dg = lambda j: [send(9, j, dg, place(sib, z))]

    def own(j):
        if j > 0:
            await_chunk(j, row)
        for copy, only_middle in by_z(j):
            guarded(only_middle, copy.start)
        for copy in in_plane(j):
            copy.start()

    def near(j):
        await_chunk(j, xn)
        for copy in from_x(j):
            copy.start()
        await_chunk(j, yn)
        for copy in from_y(j):
            copy.start()

    def along(j):
        await_chunk(j, dg, along_part, got_c)
        for copy, only_middle in dg_by_z(j):
            guarded(only_middle, copy.start)

    def diagonal(j):
        await_chunk(j, dg, top(j))
        await_chunk(j, dg, bottom(j), got_b)
        if j == 0:
            for copy, only_middle in dg_by_z(0):
                guarded(only_middle, copy.start)
        for copy in from_dg(j):
            copy.start()

    def of_core(r):
        return r + 1 - 2 * core

    def own_done(j):
        await_chunk(j, sib)
        compute(j, row, sib)

    def near_done(j):
        await_chunk(j, of_core(xn))
        compute(j, xn, of_core(xn))
        await_chunk(j, of_core(yn))
        compute(j, yn, of_core(yn))

    def diagonal_done(j):
        await_chunk(j, of_core(dg))
        compute(j, dg, of_core(dg))

    reading = pltpu.make_async_copy(res_hbm, res_ref, read)
    reading.start()
    barrier = pltpu.get_barrier_semaphore()

    def greet(to):
        pl.semaphore_signal(barrier, inc=1, device_id=to, device_id_type=pl.DeviceIdType.MESH)

    for to in (place(sib, z), place(xn, z), place(yn, z), place(row, inner)):
        greet(to)
    pl.when(middle == 1)(lambda: greet(place(row, outer)))
    held[row * n_col + z] = mine_ref[0]
    pl.semaphore_wait(barrier, 4 + middle)

    own(0)
    for g in range(NIRREP):
        pick = one_hot_rows(slot_ref, g, rows)
        amps[g] = lax.dot_general(
            amp_ref[...], pick, (((1,), (1,)), ((), ())), preferred_element_type=jnp.float32
        ).astype(jnp.bfloat16)
    reading.wait()
    own_done(0)
    own(1)
    near(0)
    own_done(1)
    own(2)
    near(1)
    near_done(0)
    diagonal(0)
    own(3)
    own_done(2)
    near_done(1)
    along(1)
    near(2)
    diagonal_done(0)
    own_done(3)
    along(2)
    diagonal(1)
    near_done(2)
    near(3)
    along(3)
    diagonal(2)
    diagonal_done(1)
    diagonal(3)
    near_done(3)
    diagonal_done(2)
    diagonal_done(3)

    for j in range(n_col):
        for r in range(n_row):
            write(r, j).wait()
        for copy, only_middle in by_z(j) + dg_by_z(j):
            guarded(only_middle, copy.wait_send)
        for copy in in_plane(j) + from_x(j) + from_y(j) + from_dg(j):
            copy.wait_send()


def spread_add(amp, slot, irrep_blk, mine, residual, n_row, n_col):
    _, rows, width = mine.shape
    parts = n_row * n_col
    vmem = pl.BlockSpec(memory_space=pltpu.VMEM)
    hbm = pl.BlockSpec(memory_space=pl.ANY)
    return pl.pallas_call(
        functools.partial(spread_kernel, per_step=width // GRAIN),
        out_shape=jax.ShapeDtypeStruct(residual.shape, jnp.bfloat16),
        in_specs=[pl.BlockSpec(memory_space=pltpu.SMEM), vmem, vmem, vmem, hbm],
        out_specs=hbm,
        scratch_shapes=[
            pltpu.VMEM((NIRREP, amp.shape[0], rows), jnp.bfloat16),
            pltpu.VMEM((parts, rows, width), jnp.bfloat16),
            pltpu.VMEM(residual.shape, jnp.bfloat16),
            pltpu.VMEM(residual.shape, jnp.bfloat16),
            pltpu.SemaphoreType.DMA((12, n_col)),
            pltpu.SemaphoreType.DMA((parts,)),
            pltpu.SemaphoreType.DMA((parts,)),
            pltpu.SemaphoreType.DMA((parts,)),
            pltpu.SemaphoreType.DMA,
            pltpu.SemaphoreType.DMA((parts,)),
        ],
        compiler_params=pltpu.CompilerParams(
            vmem_limit_bytes=48 * MIB, collective_id=0, has_side_effects=True
        ),
    )(irrep_blk, slot, amp, mine, residual)


def exchange_kernel(
    irrep_ref, slot1_ref, slot2_ref, x_ref, out_ref,
    x, mine, ours, pick1, pick2, loaded, sent, got, *, n_row, per_step
):
    row, col = lax.axis_index("row"), lax.axis_index("col")
    width = per_step * GRAIN
    cap1, cap2 = pick1.shape[1], pick2.shape[1]
    turns = list(range(1, n_row)) + [0]

    def peer(k):
        return (row + k) % n_row

    def load(k):
        cols = pl.ds(pl.multiple_of(peer(k) * width, width), width)
        return pltpu.make_async_copy(x_ref.at[:, :, cols], x.at[k], loaded.at[k])

    def send(k):
        return pltpu.make_async_remote_copy(
            src_ref=mine.at[k],
            dst_ref=ours.at[row],
            send_sem=sent.at[k],
            recv_sem=got.at[row],
            device_id={"row": peer(k), "col": col},
            device_id_type=pl.DeviceIdType.MESH,
        )

    for k in turns:
        load(k).start()
    barrier = pltpu.get_barrier_semaphore()
    for k in turns[:-1]:
        pl.semaphore_signal(
            barrier, inc=1, device_id={"row": peer(k), "col": col},
            device_id_type=pl.DeviceIdType.MESH,
        )
    for g in range(NIRREP):
        pick1[g] = one_hot_rows(slot1_ref, g, cap1)

    def pack_into(put, picks, rows, block, first):
        for t in range(0, per_step, 2):
            two = jnp.concatenate([picks[irrep_ref[first + t]], picks[irrep_ref[first + t + 1]]], axis=0)
            both = jnp.dot(
                two, block[:, t * GRAIN:(t + 2) * GRAIN], preferred_element_type=jnp.float32
            ).astype(jnp.bfloat16)
            put(t, both[:rows, :GRAIN])
            put(t + 1, both[rows:, GRAIN:])

    for k in turns:
        load(k).wait()
        block = x[k].reshape(-1, width)
        first = (col * n_row + peer(k)) * per_step

        def put(t, piece):
            cols = slice(t * GRAIN, (t + 1) * GRAIN)
            if k > 0:
                mine[k, :, cols] = piece
            else:
                ours[row, :, cols] = piece

        pack_into(put, pick1, cap1, block, first)
        if k == turns[0]:
            pl.semaphore_wait(barrier, n_row - 1)
        if k > 0:
            send(k).start()

    for g in range(NIRREP):
        pick2[g] = one_hot_rows(slot2_ref, g, cap2)
    for k in turns[:-1]:
        source = (row + n_row - k) % n_row
        pltpu.make_async_copy(mine.at[k], ours.at[source], got.at[source]).wait()

    def put_out(t, piece):
        out_ref[0, :, t * GRAIN:(t + 1) * GRAIN] = piece

    block = ours[...].reshape(n_row * cap1, width)
    pack_into(put_out, pick2, cap2, block, (col * n_row + row) * per_step)
    for k in turns[:-1]:
        send(k).wait_send()


def exchange(integrals, slot1, slot2, irrep_blk, cap1, cap2, n_row):
    steps, local_k, ab_local = integrals.shape
    width = ab_local // n_row
    vmem = pl.BlockSpec(memory_space=pltpu.VMEM)
    return pl.pallas_call(
        functools.partial(exchange_kernel, n_row=n_row, per_step=width // GRAIN),
        out_shape=jax.ShapeDtypeStruct((1, cap2, width), jnp.bfloat16),
        in_specs=[pl.BlockSpec(memory_space=pltpu.SMEM), vmem, vmem, pl.BlockSpec(memory_space=pl.ANY)],
        out_specs=vmem,
        scratch_shapes=[
            pltpu.VMEM((n_row, steps, local_k, width), jnp.bfloat16),
            pltpu.VMEM((n_row, cap1, width), jnp.bfloat16),
            pltpu.VMEM((n_row, cap1, width), jnp.bfloat16),
            pltpu.VMEM((NIRREP, cap1, steps * local_k), jnp.bfloat16),
            pltpu.VMEM((NIRREP, cap2, n_row * cap1), jnp.bfloat16),
            pltpu.SemaphoreType.DMA((n_row,)),
            pltpu.SemaphoreType.DMA((n_row,)),
            pltpu.SemaphoreType.DMA((n_row,)),
        ],
        compiler_params=pltpu.CompilerParams(
            vmem_limit_bytes=24 * MIB, collective_id=1, has_side_effects=True
        ),
    )(irrep_blk, slot1, slot2, integrals)


def per_device(n_row, n_col, amplitudes, integrals, pair_irrep, block_offset, residual):
    steps, local_k, ab_local = integrals.shape
    n1 = steps * local_k
    cap1 = round_up(-(-n1 // 3), 16)
    cap2 = round_up(-(-n1 * n_row // 6), 16)
    tight = cap2 - 16
    row, col = lax.axis_index("row"), lax.axis_index("col")

    pairs = np.arange(steps * local_k * n_row)
    holder = pairs // local_k % n_row
    same = holder[:, None] == holder[None, :]
    within = same & (pairs[:, None] <= pairs[None, :])
    ahead = holder[:, None] < holder[None, :]
    rows = np.arange(n_row)
    held = holder[:, None] == rows[None, :]
    before = holder[:, None] < rows[None, :]
    tally = np.concatenate([within, within | ahead, held, before], axis=1)
    mine = pair_irrep.reshape(1, -1) == lax.iota(jnp.int32, NIRREP)[:, None]
    sums = jnp.dot(
        mine.astype(jnp.bfloat16), jnp.asarray(tally, jnp.bfloat16),
        preferred_element_type=jnp.float32,
    ).astype(jnp.int32)
    depth = pairs.size
    rank = jnp.where(mine, sums[:, :depth] - 1, -1).reshape(NIRREP, steps, n_row, local_k)
    slot3 = jnp.where(mine, sums[:, depth:2 * depth] - 1, -1)
    count = sums[:, 2 * depth:2 * depth + n_row]
    base = sums[:, 2 * depth + n_row:]
    upto = base + count
    most = jnp.max(upto)
    level = jnp.where(
        jnp.max(count) > cap1, 2, (most > tight).astype(jnp.int32) + (most > cap2).astype(jnp.int32)
    )

    slot1 = lax.dynamic_index_in_dim(rank, row, axis=2, keepdims=False).reshape(NIRREP, n1)
    spot = lax.iota(jnp.int32, cap1)
    slot2 = jnp.where(spot[None, None] < count[:, :, None], base[:, :, None] + spot, -1)
    slot2 = slot2.reshape(NIRREP, n_row * cap1)

    blocks = n_col * ab_local // GRAIN
    starts = lax.iota(jnp.int32, blocks) * GRAIN
    irrep_blk = jnp.sum((starts[:, None] >= block_offset[None, 1:-1]).astype(jnp.int32), axis=1)

    per_col = ab_local // GRAIN

    def by_links(amplitudes, integrals, residual):
        mine = exchange(integrals, slot1, slot2, irrep_blk, cap1, tight, n_row)
        amp = amplitudes.reshape(amplitudes.shape[0], -1)
        return spread_add(amp, slot3, irrep_blk, mine, residual, n_row, n_col)

    def sparse(amplitudes, integrals, residual):
        mine1 = pack(integrals, slot1, irrep_blk, col * per_col, cap1, n_row)
        ours = lax.all_to_all(mine1, "row", split_axis=0, concat_axis=0, tiled=True)
        ours = ours.reshape(n_row * cap1, ab_local // n_row)
        first = col * per_col + row * (per_col // n_row)
        mine2 = pack(ours, slot2, irrep_blk, first, cap2, 1)
        packed = lax.all_gather(mine2, ("row", "col"), axis=0, tiled=True)
        amp = amplitudes.reshape(amplitudes.shape[0], -1)
        return ladder_add(amp, slot3, irrep_blk, packed, residual, n_row, n_col)

    def full(amplitudes, integrals, residual):
        return dense(amplitudes, integrals, pair_irrep, block_offset, residual)

    quick = by_links if (n_row, n_col) == (8, 4) else sparse
    return lax.switch(level, [quick, sparse, full], amplitudes, integrals, residual)


def solution(mesh):
    in_specs = (
        P(("row", "col"), None, None),
        P(None, "row", "col"),
        P(),
        P(),
        P(("row", "col"), None),
    )
    out_specs = P(("row", "col"), None)
    body = functools.partial(per_device, mesh.shape["row"], mesh.shape["col"])
    return jax.shard_map(
        body, mesh=mesh, in_specs=in_specs, out_specs=out_specs, check_vma=False
    )
```

```python
import functools

import jax
import jax.numpy as jnp
import numpy as np
from jax import lax
from jax.experimental import pallas as pl
from jax.experimental.pallas import tpu as pltpu
from jax.sharding import PartitionSpec as P

NIRREP = 8
GRAIN = 128
MIB = 1024 * 1024


def apply_piece(irrep_ab, amp_panel, labels, total, piece):
    kept = jnp.where(labels[:, None] == irrep_ab[None, :], piece, jnp.zeros((), piece.dtype))
    return total + jnp.dot(amp_panel, kept, preferred_element_type=jnp.float32)


def dense(amplitudes, integrals, pair_irrep, block_offset, residual):
    ab_local = integrals.shape[2]
    steps = integrals.shape[0]
    position = lax.axis_index("col") * ab_local + lax.iota(jnp.int32, ab_local)
    irrep_ab = jnp.sum((position[:, None] >= block_offset[None, 1:-1]).astype(jnp.int32), axis=1)
    grid_amps = lax.all_to_all(amplitudes, "col", split_axis=2, concat_axis=0, tiled=True)
    panels = [
        lax.all_gather(grid_amps[:, step, :], "col", axis=1, tiled=True) for step in range(steps)
    ]
    total = jnp.zeros((panels[0].shape[0], ab_local), jnp.float32)
    piece = lax.all_gather(integrals, "row", axis=1, tiled=True)
    for step in range(steps):
        total = apply_piece(irrep_ab, panels[step], pair_irrep[step], total, piece[step])
    ladder_half = total.astype(jnp.bfloat16)
    returned = lax.all_to_all(ladder_half, "col", split_axis=0, concat_axis=1, tiled=True)
    return (residual.astype(jnp.float32) + returned.astype(jnp.float32)).astype(jnp.bfloat16)


def round_up(value, grain):
    return (value + grain - 1) // grain * grain


def one_hot_rows(slot_ref, g, rows):
    width = slot_ref.shape[1]
    line = slot_ref[pl.ds(g, 1), :]
    at = lax.broadcasted_iota(jnp.int32, (rows, width), 0)
    return jnp.where(line == at, 1.0, 0.0).astype(jnp.bfloat16)


def pack_kernel(irrep_ref, slot_ref, x_ref, out_ref, pick, *, blocks, per_step):
    rows = pick.shape[1]

    @pl.when(pl.program_id(0) == 0)
    def _():
        for g in range(NIRREP):
            pick[g] = one_hot_rows(slot_ref, g, rows)

    x = x_ref[...].reshape(-1, x_ref.shape[-1])
    first = irrep_ref[blocks] + pl.program_id(0) * per_step
    for t in range(per_step):
        g = irrep_ref[first + t]
        cols = slice(t * GRAIN, (t + 1) * GRAIN)
        packed = jnp.dot(pick[g], x[:, cols], preferred_element_type=jnp.float32)
        out_ref[0, :, cols] = packed.astype(jnp.bfloat16)


def pack(x, slot, irrep_blk, first, rows, parts):
    width = x.shape[-1] // parts
    depth = slot.shape[1]
    blocks = irrep_blk.shape[0]
    scalars = jnp.concatenate([irrep_blk, first[None].astype(jnp.int32)])
    lead = x.ndim - 1
    return pl.pallas_call(
        functools.partial(pack_kernel, blocks=blocks, per_step=width // GRAIN),
        out_shape=jax.ShapeDtypeStruct((parts, rows, width), jnp.bfloat16),
        grid_spec=pltpu.PrefetchScalarGridSpec(
            num_scalar_prefetch=1,
            grid=(parts,),
            in_specs=[
                pl.BlockSpec((NIRREP, depth), lambda i, s: (0, 0)),
                pl.BlockSpec(x.shape[:-1] + (width,), lambda i, s: (0,) * lead + (i,)),
            ],
            out_specs=pl.BlockSpec((1, rows, width), lambda i, s: (i, 0, 0)),
            scratch_shapes=[pltpu.VMEM((NIRREP, rows, depth), jnp.bfloat16)],
        ),
        compiler_params=pltpu.CompilerParams(vmem_limit_bytes=24 * MIB),
    )(scalars, slot, x)


def ladder_kernel(irrep_ref, slot_ref, amp_ref, packed_ref, res_ref, out_ref, amps, *, per_step):
    rows = amps.shape[2]

    @pl.when(pl.program_id(0) == 0)
    def _():
        for g in range(NIRREP):
            pick = one_hot_rows(slot_ref, g, rows)
            amps[g] = lax.dot_general(
                amp_ref[...], pick, (((1,), (1,)), ((), ())), preferred_element_type=jnp.float32
            ).astype(jnp.bfloat16)

    first = pl.program_id(0) * per_step
    for t in range(per_step):
        g = irrep_ref[first + t]
        cols = slice(t * GRAIN, (t + 1) * GRAIN)
        ladder = jnp.dot(amps[g], packed_ref[0, :, cols], preferred_element_type=jnp.float32)
        ladder = ladder.astype(jnp.bfloat16).astype(jnp.float32)
        out_ref[:, cols] = (res_ref[:, cols].astype(jnp.float32) + ladder).astype(jnp.bfloat16)


def ladder_add(amp, slot, irrep_blk, packed, residual, n_row, n_col):
    parts, rows, width = packed.shape
    pairs, depth = amp.shape
    return pl.pallas_call(
        functools.partial(ladder_kernel, per_step=width // GRAIN),
        out_shape=jax.ShapeDtypeStruct(residual.shape, jnp.bfloat16),
        grid_spec=pltpu.PrefetchScalarGridSpec(
            num_scalar_prefetch=1,
            grid=(parts,),
            in_specs=[
                pl.BlockSpec((NIRREP, depth), lambda i, s: (0, 0)),
                pl.BlockSpec((pairs, depth), lambda i, s: (0, 0)),
                pl.BlockSpec((1, rows, width), lambda i, s: ((i % n_row) * n_col + i // n_row, 0, 0)),
                pl.BlockSpec((pairs, width), lambda i, s: (0, i)),
            ],
            out_specs=pl.BlockSpec((pairs, width), lambda i, s: (0, i)),
            scratch_shapes=[pltpu.VMEM((NIRREP, pairs, rows), jnp.bfloat16)],
        ),
        compiler_params=pltpu.CompilerParams(vmem_limit_bytes=24 * MIB),
    )(irrep_blk, slot, amp, packed, residual)


def spread_kernel(
    irrep_ref, slot_ref, amp_ref, mine_ref, res_hbm, out_hbm,
    amps, held, res_ref, out_ref, sent, got, got_b, got_c, read, wrote, *, per_step
):
    n_row, n_col = 8, 4
    row, z = lax.axis_index("row"), lax.axis_index("col")
    pairs, padded, rows = amp_ref.shape[0], amps.shape[1], amps.shape[2]
    half = round_up(rows // 2, 16)
    along_rows = rows - 32
    along_part = pl.ds(0, along_rows)

    def top(j):
        return pl.ds(0, half) if j == 0 else pl.ds(along_rows, 16)

    def bottom(j):
        return pl.ds(half, rows - half) if j == 0 else pl.ds(along_rows + 16, 16)

    core, x, y = row % 2, (row // 2) % 2, row // 4
    sib = row + 1 - 2 * core
    xn = row + 2 - 4 * x
    yn = row + 4 - 8 * y
    dg = xn + 4 - 8 * y
    far = z // 2
    middle = z + far * (3 - 2 * z)
    order = [middle, 1 - middle, 2, 3]
    order = [o + far * (3 - 2 * o) for o in order]
    inner = z + 1 - 2 * far
    outer = z - 1 + 2 * far

    def place(r, c):
        return {"row": r, "col": c}

    def send(kind, j, r, to, part=None, recv=got):
        slot = r * n_col + order[j]
        ref = held.at[slot] if part is None else held.at[slot, part]
        return pltpu.make_async_remote_copy(
            src_ref=ref,
            dst_ref=ref,
            send_sem=sent.at[kind, j],
            recv_sem=recv.at[slot],
            device_id=to,
            device_id_type=pl.DeviceIdType.MESH,
        )

    def await_chunk(j, r, part=None, recv=got):
        send(0, j, r, place(sib, z), part, recv).wait_recv()

    def write(r, c):
        width = per_step * GRAIN
        cols = pl.ds(pl.multiple_of((c * n_row + r) * width, width), width)
        return pltpu.make_async_copy(out_ref.at[:, cols], out_hbm.at[:, cols], wrote.at[r * n_col + c])

    def compute(j, r_first, r_other):
        def body(i, carry):
            r = r_first + i * (r_other - r_first)
            chunk = order[j] * n_row + r
            slot = r * n_col + order[j]
            for t in range(0, per_step, 2):
                block = chunk * per_step + t
                two = jnp.concatenate([amps[irrep_ref[block]], amps[irrep_ref[block + 1]]], axis=0)
                cols = pl.ds(pl.multiple_of(block * GRAIN, 2 * GRAIN), 2 * GRAIN)
                piece = held[slot, :, t * GRAIN:(t + 2) * GRAIN]
                both = jnp.dot(two, piece, preferred_element_type=jnp.float32)
                ladder = jnp.concatenate(
                    [both[:pairs, :GRAIN], both[padded:padded + pairs, GRAIN:]], axis=1
                )
                ladder = ladder.astype(jnp.bfloat16).astype(jnp.float32)
                total = res_ref[:, cols].astype(jnp.float32) + ladder
                out_ref[:, cols] = total.astype(jnp.bfloat16)
            write(r, order[j]).start()
            return carry

        lax.fori_loop(0, 2, body, 0)

    def by_z(j, r=row, part=None, recv=got, kind=0):
        if j == 0:
            return [
                (send(kind, 0, r, place(row, inner), part, recv), False),
                (send(kind + 1, 0, r, place(row, outer), part, recv), True),
            ]
        to = inner if j == 1 else outer
        return [(send(kind if j == 1 else kind + 1, j, r, place(row, to), part, recv), True)]

    def dg_by_z(j):
        return by_z(j, dg, along_part, got_c, 10)

    def guarded(only_middle, act):
        if only_middle:
            pl.when(middle == 1)(act)
        else:
            act()

    in_plane = lambda j: [
        send(2, j, row, place(xn, z)),
        send(3, j, row, place(yn, z)),
        send(4, j, row, place(sib, z)),
    ]
    from_x = lambda j: [
        send(5, j, xn, place(yn, z), top(j)),
        send(7, j, xn, place(sib, z)),
    ]
    from_y = lambda j: [
        send(6, j, yn, place(xn, z), bottom(j), got_b),
        send(8, j, yn, place(sib, z)),
    ]
    from_dg = lambda j: [send(9, j, dg, place(sib, z))]

    def own(j):
        if j > 0:
            await_chunk(j, row)
        for copy, only_middle in by_z(j):
            guarded(only_middle, copy.start)
        for copy in in_plane(j):
            copy.start()

    def near(j):
        await_chunk(j, xn)
        for copy in from_x(j):
            copy.start()
        await_chunk(j, yn)
        for copy in from_y(j):
            copy.start()

    def along(j):
        await_chunk(j, dg, along_part, got_c)
        for copy, only_middle in dg_by_z(j):
            guarded(only_middle, copy.start)

    def diagonal(j):
        await_chunk(j, dg, top(j))
        await_chunk(j, dg, bottom(j), got_b)
        if j == 0:
            for copy, only_middle in dg_by_z(0):
                guarded(only_middle, copy.start)
        for copy in from_dg(j):
            copy.start()

    def of_core(r):
        return r + 1 - 2 * core

    def own_done(j):
        await_chunk(j, sib)
        compute(j, row, sib)

    def near_done(j):
        await_chunk(j, of_core(xn))
        compute(j, xn, of_core(xn))
        await_chunk(j, of_core(yn))
        compute(j, yn, of_core(yn))

    def diagonal_done(j):
        await_chunk(j, of_core(dg))
        compute(j, dg, of_core(dg))

    reading = pltpu.make_async_copy(res_hbm, res_ref, read)
    reading.start()
    barrier = pltpu.get_barrier_semaphore()

    def greet(to):
        pl.semaphore_signal(barrier, inc=1, device_id=to, device_id_type=pl.DeviceIdType.MESH)

    for to in (place(sib, z), place(xn, z), place(yn, z), place(row, inner)):
        greet(to)
    pl.when(middle == 1)(lambda: greet(place(row, outer)))
    held[row * n_col + z] = mine_ref[0]
    pl.semaphore_wait(barrier, 4 + middle)

    own(0)
    amps[...] = jnp.zeros_like(amps)
    for g in range(NIRREP):
        pick = one_hot_rows(slot_ref, g, rows)
        amps[g, :pairs, :] = lax.dot_general(
            amp_ref[...], pick, (((1,), (1,)), ((), ())), preferred_element_type=jnp.float32
        ).astype(jnp.bfloat16)
    reading.wait()
    own_done(0)
    own(1)
    near(0)
    own_done(1)
    own(2)
    near(1)
    near_done(0)
    diagonal(0)
    own(3)
    own_done(2)
    near_done(1)
    along(1)
    near(2)
    diagonal_done(0)
    own_done(3)
    along(2)
    diagonal(1)
    near_done(2)
    near(3)
    along(3)
    diagonal(2)
    diagonal_done(1)
    diagonal(3)
    near_done(3)
    diagonal_done(2)
    diagonal_done(3)

    for j in range(n_col):
        for r in range(n_row):
            write(r, j).wait()
        for copy, only_middle in by_z(j) + dg_by_z(j):
            guarded(only_middle, copy.wait_send)
        for copy in in_plane(j) + from_x(j) + from_y(j) + from_dg(j):
            copy.wait_send()


def spread_add(amp, slot, irrep_blk, mine, residual, n_row, n_col):
    _, rows, width = mine.shape
    parts = n_row * n_col
    vmem = pl.BlockSpec(memory_space=pltpu.VMEM)
    hbm = pl.BlockSpec(memory_space=pl.ANY)
    return pl.pallas_call(
        functools.partial(spread_kernel, per_step=width // GRAIN),
        out_shape=jax.ShapeDtypeStruct(residual.shape, jnp.bfloat16),
        in_specs=[pl.BlockSpec(memory_space=pltpu.SMEM), vmem, vmem, vmem, hbm],
        out_specs=hbm,
        scratch_shapes=[
            pltpu.VMEM((NIRREP, round_up(amp.shape[0], 16), rows), jnp.bfloat16),
            pltpu.VMEM((parts, rows, width), jnp.bfloat16),
            pltpu.VMEM(residual.shape, jnp.bfloat16),
            pltpu.VMEM(residual.shape, jnp.bfloat16),
            pltpu.SemaphoreType.DMA((12, n_col)),
            pltpu.SemaphoreType.DMA((parts,)),
            pltpu.SemaphoreType.DMA((parts,)),
            pltpu.SemaphoreType.DMA((parts,)),
            pltpu.SemaphoreType.DMA,
            pltpu.SemaphoreType.DMA((parts,)),
        ],
        compiler_params=pltpu.CompilerParams(
            vmem_limit_bytes=48 * MIB, collective_id=0, has_side_effects=True
        ),
    )(irrep_blk, slot, amp, mine, residual)


def exchange_kernel(
    irrep_ref, slot1_ref, slot2_ref, x_ref, out_ref,
    x, mine, ours, pick1, pick2, loaded, sent, got, *, n_row, per_step
):
    row, col = lax.axis_index("row"), lax.axis_index("col")
    width = per_step * GRAIN
    cap1, cap2 = pick1.shape[1], pick2.shape[1]
    turns = list(range(1, n_row)) + [0]

    def peer(k):
        return (row + k) % n_row

    def load(k):
        cols = pl.ds(pl.multiple_of(peer(k) * width, width), width)
        return pltpu.make_async_copy(x_ref.at[:, :, cols], x.at[k], loaded.at[k])

    def send(k):
        return pltpu.make_async_remote_copy(
            src_ref=mine.at[k],
            dst_ref=ours.at[row],
            send_sem=sent.at[k],
            recv_sem=got.at[row],
            device_id={"row": peer(k), "col": col},
            device_id_type=pl.DeviceIdType.MESH,
        )

    for k in turns:
        load(k).start()
    barrier = pltpu.get_barrier_semaphore()
    for k in turns[:-1]:
        pl.semaphore_signal(
            barrier, inc=1, device_id={"row": peer(k), "col": col},
            device_id_type=pl.DeviceIdType.MESH,
        )
    for g in range(NIRREP):
        pick1[g] = one_hot_rows(slot1_ref, g, cap1)

    def pack_into(put, picks, rows, block, first):
        for t in range(0, per_step, 2):
            two = jnp.concatenate([picks[irrep_ref[first + t]], picks[irrep_ref[first + t + 1]]], axis=0)
            both = jnp.dot(
                two, block[:, t * GRAIN:(t + 2) * GRAIN], preferred_element_type=jnp.float32
            ).astype(jnp.bfloat16)
            put(t, both[:rows, :GRAIN])
            put(t + 1, both[rows:, GRAIN:])

    for k in turns:
        load(k).wait()
        block = x[k].reshape(-1, width)
        first = (col * n_row + peer(k)) * per_step

        def put(t, piece):
            cols = slice(t * GRAIN, (t + 1) * GRAIN)
            if k > 0:
                mine[k, :, cols] = piece
            else:
                ours[row, :, cols] = piece

        pack_into(put, pick1, cap1, block, first)
        if k == turns[0]:
            pl.semaphore_wait(barrier, n_row - 1)
        if k > 0:
            send(k).start()

    for g in range(NIRREP):
        pick2[g] = one_hot_rows(slot2_ref, g, cap2)
    for k in turns[:-1]:
        source = (row + n_row - k) % n_row
        pltpu.make_async_copy(mine.at[k], ours.at[source], got.at[source]).wait()

    def put_out(t, piece):
        out_ref[0, :, t * GRAIN:(t + 1) * GRAIN] = piece

    block = ours[...].reshape(n_row * cap1, width)
    pack_into(put_out, pick2, cap2, block, (col * n_row + row) * per_step)
    for k in turns[:-1]:
        send(k).wait_send()


def exchange(integrals, slot1, slot2, irrep_blk, cap1, cap2, n_row):
    steps, local_k, ab_local = integrals.shape
    width = ab_local // n_row
    vmem = pl.BlockSpec(memory_space=pltpu.VMEM)
    return pl.pallas_call(
        functools.partial(exchange_kernel, n_row=n_row, per_step=width // GRAIN),
        out_shape=jax.ShapeDtypeStruct((1, cap2, width), jnp.bfloat16),
        in_specs=[pl.BlockSpec(memory_space=pltpu.SMEM), vmem, vmem, pl.BlockSpec(memory_space=pl.ANY)],
        out_specs=vmem,
        scratch_shapes=[
            pltpu.VMEM((n_row, steps, local_k, width), jnp.bfloat16),
            pltpu.VMEM((n_row, cap1, width), jnp.bfloat16),
            pltpu.VMEM((n_row, cap1, width), jnp.bfloat16),
            pltpu.VMEM((NIRREP, cap1, steps * local_k), jnp.bfloat16),
            pltpu.VMEM((NIRREP, cap2, n_row * cap1), jnp.bfloat16),
            pltpu.SemaphoreType.DMA((n_row,)),
            pltpu.SemaphoreType.DMA((n_row,)),
            pltpu.SemaphoreType.DMA((n_row,)),
        ],
        compiler_params=pltpu.CompilerParams(
            vmem_limit_bytes=24 * MIB, collective_id=1, has_side_effects=True
        ),
    )(irrep_blk, slot1, slot2, integrals)


def per_device(n_row, n_col, amplitudes, integrals, pair_irrep, block_offset, residual):
    steps, local_k, ab_local = integrals.shape
    n1 = steps * local_k
    cap1 = round_up(-(-n1 // 3), 16)
    cap2 = round_up(-(-n1 * n_row // 6), 16)
    tight = cap2 - 16
    row, col = lax.axis_index("row"), lax.axis_index("col")

    pairs = np.arange(steps * local_k * n_row)
    holder = pairs // local_k % n_row
    same = holder[:, None] == holder[None, :]
    within = same & (pairs[:, None] <= pairs[None, :])
    ahead = holder[:, None] < holder[None, :]
    rows = np.arange(n_row)
    held = holder[:, None] == rows[None, :]
    before = holder[:, None] < rows[None, :]
    tally = np.concatenate([within, within | ahead, held, before], axis=1)
    mine = pair_irrep.reshape(1, -1) == lax.iota(jnp.int32, NIRREP)[:, None]
    sums = jnp.dot(
        mine.astype(jnp.bfloat16), jnp.asarray(tally, jnp.bfloat16),
        preferred_element_type=jnp.float32,
    ).astype(jnp.int32)
    depth = pairs.size
    rank = jnp.where(mine, sums[:, :depth] - 1, -1).reshape(NIRREP, steps, n_row, local_k)
    slot3 = jnp.where(mine, sums[:, depth:2 * depth] - 1, -1)
    count = sums[:, 2 * depth:2 * depth + n_row]
    base = sums[:, 2 * depth + n_row:]
    upto = base + count
    most = jnp.max(upto)
    level = jnp.where(
        jnp.max(count) > cap1, 2, (most > tight).astype(jnp.int32) + (most > cap2).astype(jnp.int32)
    )

    slot1 = lax.dynamic_index_in_dim(rank, row, axis=2, keepdims=False).reshape(NIRREP, n1)
    spot = lax.iota(jnp.int32, cap1)
    slot2 = jnp.where(spot[None, None] < count[:, :, None], base[:, :, None] + spot, -1)
    slot2 = slot2.reshape(NIRREP, n_row * cap1)

    blocks = n_col * ab_local // GRAIN
    starts = lax.iota(jnp.int32, blocks) * GRAIN
    irrep_blk = jnp.sum((starts[:, None] >= block_offset[None, 1:-1]).astype(jnp.int32), axis=1)

    per_col = ab_local // GRAIN

    def by_links(amplitudes, integrals, residual):
        mine = exchange(integrals, slot1, slot2, irrep_blk, cap1, tight, n_row)
        amp = amplitudes.reshape(amplitudes.shape[0], -1)
        return spread_add(amp, slot3, irrep_blk, mine, residual, n_row, n_col)

    def sparse(amplitudes, integrals, residual):
        mine1 = pack(integrals, slot1, irrep_blk, col * per_col, cap1, n_row)
        ours = lax.all_to_all(mine1, "row", split_axis=0, concat_axis=0, tiled=True)
        ours = ours.reshape(n_row * cap1, ab_local // n_row)
        first = col * per_col + row * (per_col // n_row)
        mine2 = pack(ours, slot2, irrep_blk, first, cap2, 1)
        packed = lax.all_gather(mine2, ("row", "col"), axis=0, tiled=True)
        amp = amplitudes.reshape(amplitudes.shape[0], -1)
        return ladder_add(amp, slot3, irrep_blk, packed, residual, n_row, n_col)

    def full(amplitudes, integrals, residual):
        return dense(amplitudes, integrals, pair_irrep, block_offset, residual)

    quick = by_links if (n_row, n_col) == (8, 4) else sparse
    return lax.switch(level, [quick, sparse, full], amplitudes, integrals, residual)


def solution(mesh):
    in_specs = (
        P(("row", "col"), None, None),
        P(None, "row", "col"),
        P(),
        P(),
        P(("row", "col"), None),
    )
    out_specs = P(("row", "col"), None)
    body = functools.partial(per_device, mesh.shape["row"], mesh.shape["col"])
    return jax.shard_map(
        body, mesh=mesh, in_specs=in_specs, out_specs=out_specs, check_vma=False
    )
```

```python
import functools

import jax
import jax.numpy as jnp
import numpy as np
from jax import lax
from jax.experimental import pallas as pl
from jax.experimental.pallas import tpu as pltpu
from jax.sharding import PartitionSpec as P

NIRREP = 8
GRAIN = 128
MIB = 1024 * 1024


def apply_piece(irrep_ab, amp_panel, labels, total, piece):
    kept = jnp.where(labels[:, None] == irrep_ab[None, :], piece, jnp.zeros((), piece.dtype))
    return total + jnp.dot(amp_panel, kept, preferred_element_type=jnp.float32)


def dense(amplitudes, integrals, pair_irrep, block_offset, residual):
    ab_local = integrals.shape[2]
    steps = integrals.shape[0]
    position = lax.axis_index("col") * ab_local + lax.iota(jnp.int32, ab_local)
    irrep_ab = jnp.sum((position[:, None] >= block_offset[None, 1:-1]).astype(jnp.int32), axis=1)
    grid_amps = lax.all_to_all(amplitudes, "col", split_axis=2, concat_axis=0, tiled=True)
    panels = [
        lax.all_gather(grid_amps[:, step, :], "col", axis=1, tiled=True) for step in range(steps)
    ]
    total = jnp.zeros((panels[0].shape[0], ab_local), jnp.float32)
    piece = lax.all_gather(integrals, "row", axis=1, tiled=True)
    for step in range(steps):
        total = apply_piece(irrep_ab, panels[step], pair_irrep[step], total, piece[step])
    ladder_half = total.astype(jnp.bfloat16)
    returned = lax.all_to_all(ladder_half, "col", split_axis=0, concat_axis=1, tiled=True)
    return (residual.astype(jnp.float32) + returned.astype(jnp.float32)).astype(jnp.bfloat16)


def round_up(value, grain):
    return (value + grain - 1) // grain * grain


def one_hot_rows(slot_ref, g, rows):
    width = slot_ref.shape[1]
    line = slot_ref[pl.ds(g, 1), :]
    at = lax.broadcasted_iota(jnp.int32, (rows, width), 0)
    return jnp.where(line == at, 1.0, 0.0).astype(jnp.bfloat16)


def pack_kernel(irrep_ref, slot_ref, x_ref, out_ref, pick, *, blocks, per_step):
    rows = pick.shape[1]

    @pl.when(pl.program_id(0) == 0)
    def _():
        for g in range(NIRREP):
            pick[g] = one_hot_rows(slot_ref, g, rows)

    x = x_ref[...].reshape(-1, x_ref.shape[-1])
    first = irrep_ref[blocks] + pl.program_id(0) * per_step
    for t in range(per_step):
        g = irrep_ref[first + t]
        cols = slice(t * GRAIN, (t + 1) * GRAIN)
        packed = jnp.dot(pick[g], x[:, cols], preferred_element_type=jnp.float32)
        out_ref[0, :, cols] = packed.astype(jnp.bfloat16)


def pack(x, slot, irrep_blk, first, rows, parts):
    width = x.shape[-1] // parts
    depth = slot.shape[1]
    blocks = irrep_blk.shape[0]
    scalars = jnp.concatenate([irrep_blk, first[None].astype(jnp.int32)])
    lead = x.ndim - 1
    return pl.pallas_call(
        functools.partial(pack_kernel, blocks=blocks, per_step=width // GRAIN),
        out_shape=jax.ShapeDtypeStruct((parts, rows, width), jnp.bfloat16),
        grid_spec=pltpu.PrefetchScalarGridSpec(
            num_scalar_prefetch=1,
            grid=(parts,),
            in_specs=[
                pl.BlockSpec((NIRREP, depth), lambda i, s: (0, 0)),
                pl.BlockSpec(x.shape[:-1] + (width,), lambda i, s: (0,) * lead + (i,)),
            ],
            out_specs=pl.BlockSpec((1, rows, width), lambda i, s: (i, 0, 0)),
            scratch_shapes=[pltpu.VMEM((NIRREP, rows, depth), jnp.bfloat16)],
        ),
        compiler_params=pltpu.CompilerParams(vmem_limit_bytes=24 * MIB),
    )(scalars, slot, x)


def ladder_kernel(irrep_ref, slot_ref, amp_ref, packed_ref, res_ref, out_ref, amps, *, per_step):
    rows = amps.shape[2]

    @pl.when(pl.program_id(0) == 0)
    def _():
        for g in range(NIRREP):
            pick = one_hot_rows(slot_ref, g, rows)
            amps[g] = lax.dot_general(
                amp_ref[...], pick, (((1,), (1,)), ((), ())), preferred_element_type=jnp.float32
            ).astype(jnp.bfloat16)

    first = pl.program_id(0) * per_step
    for t in range(per_step):
        g = irrep_ref[first + t]
        cols = slice(t * GRAIN, (t + 1) * GRAIN)
        ladder = jnp.dot(amps[g], packed_ref[0, :, cols], preferred_element_type=jnp.float32)
        ladder = ladder.astype(jnp.bfloat16).astype(jnp.float32)
        out_ref[:, cols] = (res_ref[:, cols].astype(jnp.float32) + ladder).astype(jnp.bfloat16)


def ladder_add(amp, slot, irrep_blk, packed, residual, n_row, n_col):
    parts, rows, width = packed.shape
    pairs, depth = amp.shape
    return pl.pallas_call(
        functools.partial(ladder_kernel, per_step=width // GRAIN),
        out_shape=jax.ShapeDtypeStruct(residual.shape, jnp.bfloat16),
        grid_spec=pltpu.PrefetchScalarGridSpec(
            num_scalar_prefetch=1,
            grid=(parts,),
            in_specs=[
                pl.BlockSpec((NIRREP, depth), lambda i, s: (0, 0)),
                pl.BlockSpec((pairs, depth), lambda i, s: (0, 0)),
                pl.BlockSpec((1, rows, width), lambda i, s: ((i % n_row) * n_col + i // n_row, 0, 0)),
                pl.BlockSpec((pairs, width), lambda i, s: (0, i)),
            ],
            out_specs=pl.BlockSpec((pairs, width), lambda i, s: (0, i)),
            scratch_shapes=[pltpu.VMEM((NIRREP, pairs, rows), jnp.bfloat16)],
        ),
        compiler_params=pltpu.CompilerParams(vmem_limit_bytes=24 * MIB),
    )(irrep_blk, slot, amp, packed, residual)


def spread_kernel(
    irrep_ref, slot_ref, amp_ref, mine_ref, res_hbm, out_hbm,
    amps, held, res_ref, out_ref, sent, got, got_b, got_c, read, wrote, *, per_step
):
    n_row, n_col = 8, 4
    row, z = lax.axis_index("row"), lax.axis_index("col")
    pairs, padded, rows = amp_ref.shape[0], amps.shape[1], amps.shape[2]
    half = round_up(rows // 2, 16)
    along_rows = rows - 32
    along_part = pl.ds(0, along_rows)

    def top(j):
        return pl.ds(0, half) if j == 0 else pl.ds(along_rows, 16)

    def bottom(j):
        return pl.ds(half, rows - half) if j == 0 else pl.ds(along_rows + 16, 16)

    core, x, y = row % 2, (row // 2) % 2, row // 4
    sib = row + 1 - 2 * core
    xn = row + 2 - 4 * x
    yn = row + 4 - 8 * y
    dg = xn + 4 - 8 * y
    far = z // 2
    middle = z + far * (3 - 2 * z)
    order = [middle, 1 - middle, 2, 3]
    order = [o + far * (3 - 2 * o) for o in order]
    inner = z + 1 - 2 * far
    outer = z - 1 + 2 * far

    def place(r, c):
        return {"row": r, "col": c}

    def send(kind, j, r, to, part=None, recv=got):
        slot = r * n_col + order[j]
        ref = held.at[slot] if part is None else held.at[slot, part]
        return pltpu.make_async_remote_copy(
            src_ref=ref,
            dst_ref=ref,
            send_sem=sent.at[kind, j],
            recv_sem=recv.at[slot],
            device_id=to,
            device_id_type=pl.DeviceIdType.MESH,
        )

    def await_chunk(j, r, part=None, recv=got):
        send(0, j, r, place(sib, z), part, recv).wait_recv()

    def write(r, c):
        width = per_step * GRAIN
        cols = pl.ds(pl.multiple_of((c * n_row + r) * width, width), width)
        return pltpu.make_async_copy(out_ref.at[:, cols], out_hbm.at[:, cols], wrote.at[r * n_col + c])

    def compute(j, r_first, r_other):
        def body(i, carry):
            r = r_first + i * (r_other - r_first)
            chunk = order[j] * n_row + r
            slot = r * n_col + order[j]
            for t in range(0, per_step, 2):
                block = chunk * per_step + t
                two = jnp.concatenate([amps[irrep_ref[block]], amps[irrep_ref[block + 1]]], axis=0)
                cols = pl.ds(pl.multiple_of(block * GRAIN, 2 * GRAIN), 2 * GRAIN)
                piece = held[slot, :, t * GRAIN:(t + 2) * GRAIN]
                both = jnp.dot(two, piece, preferred_element_type=jnp.float32)
                ladder = jnp.concatenate(
                    [both[:pairs, :GRAIN], both[padded:padded + pairs, GRAIN:]], axis=1
                )
                ladder = ladder.astype(jnp.bfloat16).astype(jnp.float32)
                total = res_ref[:, cols].astype(jnp.float32) + ladder
                out_ref[:, cols] = total.astype(jnp.bfloat16)
            write(r, order[j]).start()
            return carry

        lax.fori_loop(0, 2, body, 0)

    def by_z(j, r=row, part=None, recv=got, kind=0):
        if j == 0:
            return [
                (send(kind, 0, r, place(row, inner), part, recv), False),
                (send(kind + 1, 0, r, place(row, outer), part, recv), True),
            ]
        to = inner if j == 1 else outer
        return [(send(kind if j == 1 else kind + 1, j, r, place(row, to), part, recv), True)]

    def dg_by_z(j):
        return by_z(j, dg, along_part, got_c, 10)

    def guarded(only_middle, act):
        if only_middle:
            pl.when(middle == 1)(act)
        else:
            act()

    in_plane = lambda j: [
        send(2, j, row, place(xn, z)),
        send(3, j, row, place(yn, z)),
        send(4, j, row, place(sib, z)),
    ]
    from_x = lambda j: [
        send(5, j, xn, place(yn, z), top(j)),
        send(7, j, xn, place(sib, z)),
    ]
    from_y = lambda j: [
        send(6, j, yn, place(xn, z), bottom(j), got_b),
        send(8, j, yn, place(sib, z)),
    ]
    from_dg = lambda j: [send(9, j, dg, place(sib, z))]

    def own(j):
        if j > 0:
            await_chunk(j, row)
        for copy, only_middle in by_z(j):
            guarded(only_middle, copy.start)
        for copy in in_plane(j):
            copy.start()

    def near(j):
        await_chunk(j, xn)
        for copy in from_x(j):
            copy.start()
        await_chunk(j, yn)
        for copy in from_y(j):
            copy.start()

    def along(j):
        await_chunk(j, dg, along_part, got_c)
        for copy, only_middle in dg_by_z(j):
            guarded(only_middle, copy.start)

    def diagonal(j):
        await_chunk(j, dg, top(j))
        await_chunk(j, dg, bottom(j), got_b)
        if j == 0:
            for copy, only_middle in dg_by_z(0):
                guarded(only_middle, copy.start)
        for copy in from_dg(j):
            copy.start()

    def of_core(r):
        return r + 1 - 2 * core

    def own_done(j):
        await_chunk(j, sib)
        compute(j, row, sib)

    def near_done(j):
        await_chunk(j, of_core(xn))
        compute(j, xn, of_core(xn))
        await_chunk(j, of_core(yn))
        compute(j, yn, of_core(yn))

    def diagonal_done(j):
        await_chunk(j, of_core(dg))
        compute(j, dg, of_core(dg))

    reading = pltpu.make_async_copy(res_hbm, res_ref, read)
    reading.start()
    barrier = pltpu.get_barrier_semaphore()

    def greet(to):
        pl.semaphore_signal(barrier, inc=1, device_id=to, device_id_type=pl.DeviceIdType.MESH)

    for to in (place(sib, z), place(xn, z), place(yn, z), place(row, inner)):
        greet(to)
    pl.when(middle == 1)(lambda: greet(place(row, outer)))
    held[row * n_col + z] = mine_ref[0]
    pl.semaphore_wait(barrier, 4 + middle)

    own(0)
    amps[...] = jnp.zeros_like(amps)
    for g in range(NIRREP):
        pick = one_hot_rows(slot_ref, g, rows)
        amps[g, :pairs, :] = lax.dot_general(
            amp_ref[...], pick, (((1,), (1,)), ((), ())), preferred_element_type=jnp.float32
        ).astype(jnp.bfloat16)
    reading.wait()
    near(0)
    own(1)
    own_done(0)
    diagonal(0)
    own(2)
    near(1)
    own_done(1)
    near_done(0)
    along(1)
    own(3)
    diagonal_done(0)
    own_done(2)
    near(2)
    along(2)
    diagonal(1)
    near_done(1)
    own_done(3)
    near(3)
    along(3)
    diagonal(2)
    near_done(2)
    diagonal_done(1)
    diagonal(3)
    near_done(3)
    diagonal_done(2)
    diagonal_done(3)

    for j in range(n_col):
        for r in range(n_row):
            write(r, j).wait()
        for copy, only_middle in by_z(j) + dg_by_z(j):
            guarded(only_middle, copy.wait_send)
        for copy in in_plane(j) + from_x(j) + from_y(j) + from_dg(j):
            copy.wait_send()


def spread_add(amp, slot, irrep_blk, mine, residual, n_row, n_col):
    _, rows, width = mine.shape
    parts = n_row * n_col
    vmem = pl.BlockSpec(memory_space=pltpu.VMEM)
    hbm = pl.BlockSpec(memory_space=pl.ANY)
    return pl.pallas_call(
        functools.partial(spread_kernel, per_step=width // GRAIN),
        out_shape=jax.ShapeDtypeStruct(residual.shape, jnp.bfloat16),
        in_specs=[pl.BlockSpec(memory_space=pltpu.SMEM), vmem, vmem, vmem, hbm],
        out_specs=hbm,
        scratch_shapes=[
            pltpu.VMEM((NIRREP, round_up(amp.shape[0], 16), rows), jnp.bfloat16),
            pltpu.VMEM((parts, rows, width), jnp.bfloat16),
            pltpu.VMEM(residual.shape, jnp.bfloat16),
            pltpu.VMEM(residual.shape, jnp.bfloat16),
            pltpu.SemaphoreType.DMA((12, n_col)),
            pltpu.SemaphoreType.DMA((parts,)),
            pltpu.SemaphoreType.DMA((parts,)),
            pltpu.SemaphoreType.DMA((parts,)),
            pltpu.SemaphoreType.DMA,
            pltpu.SemaphoreType.DMA((parts,)),
        ],
        compiler_params=pltpu.CompilerParams(
            vmem_limit_bytes=48 * MIB, collective_id=0, has_side_effects=True
        ),
    )(irrep_blk, slot, amp, mine, residual)


def exchange_kernel(
    irrep_ref, slot1_ref, slot2_ref, x_ref, out_ref,
    x, mine, ours, pick1, pick2, loaded, sent, got, *, n_row, per_step
):
    row, col = lax.axis_index("row"), lax.axis_index("col")
    width = per_step * GRAIN
    cap1, cap2 = pick1.shape[1], pick2.shape[1]
    turns = list(range(1, n_row)) + [0]

    def peer(k):
        return (row + k) % n_row

    def load(k):
        cols = pl.ds(pl.multiple_of(peer(k) * width, width), width)
        return pltpu.make_async_copy(x_ref.at[:, :, cols], x.at[k], loaded.at[k])

    def send(k):
        return pltpu.make_async_remote_copy(
            src_ref=mine.at[k],
            dst_ref=ours.at[row],
            send_sem=sent.at[k],
            recv_sem=got.at[row],
            device_id={"row": peer(k), "col": col},
            device_id_type=pl.DeviceIdType.MESH,
        )

    for k in turns:
        load(k).start()
    barrier = pltpu.get_barrier_semaphore()
    for k in turns[:-1]:
        pl.semaphore_signal(
            barrier, inc=1, device_id={"row": peer(k), "col": col},
            device_id_type=pl.DeviceIdType.MESH,
        )
    for g in range(NIRREP):
        pick1[g] = one_hot_rows(slot1_ref, g, cap1)

    def pack_into(put, picks, rows, block, first):
        for t in range(0, per_step, 2):
            two = jnp.concatenate([picks[irrep_ref[first + t]], picks[irrep_ref[first + t + 1]]], axis=0)
            both = jnp.dot(
                two, block[:, t * GRAIN:(t + 2) * GRAIN], preferred_element_type=jnp.float32
            ).astype(jnp.bfloat16)
            put(t, both[:rows, :GRAIN])
            put(t + 1, both[rows:, GRAIN:])

    for k in turns:
        load(k).wait()
        block = x[k].reshape(-1, width)
        first = (col * n_row + peer(k)) * per_step

        def put(t, piece):
            cols = slice(t * GRAIN, (t + 1) * GRAIN)
            if k > 0:
                mine[k, :, cols] = piece
            else:
                ours[row, :, cols] = piece

        pack_into(put, pick1, cap1, block, first)
        if k == turns[0]:
            pl.semaphore_wait(barrier, n_row - 1)
        if k > 0:
            send(k).start()

    for g in range(NIRREP):
        pick2[g] = one_hot_rows(slot2_ref, g, cap2)
    for k in turns[:-1]:
        source = (row + n_row - k) % n_row
        pltpu.make_async_copy(mine.at[k], ours.at[source], got.at[source]).wait()

    def put_out(t, piece):
        out_ref[0, :, t * GRAIN:(t + 1) * GRAIN] = piece

    block = ours[...].reshape(n_row * cap1, width)
    pack_into(put_out, pick2, cap2, block, (col * n_row + row) * per_step)
    for k in turns[:-1]:
        send(k).wait_send()


def exchange(integrals, slot1, slot2, irrep_blk, cap1, cap2, n_row):
    steps, local_k, ab_local = integrals.shape
    width = ab_local // n_row
    vmem = pl.BlockSpec(memory_space=pltpu.VMEM)
    return pl.pallas_call(
        functools.partial(exchange_kernel, n_row=n_row, per_step=width // GRAIN),
        out_shape=jax.ShapeDtypeStruct((1, cap2, width), jnp.bfloat16),
        in_specs=[pl.BlockSpec(memory_space=pltpu.SMEM), vmem, vmem, pl.BlockSpec(memory_space=pl.ANY)],
        out_specs=vmem,
        scratch_shapes=[
            pltpu.VMEM((n_row, steps, local_k, width), jnp.bfloat16),
            pltpu.VMEM((n_row, cap1, width), jnp.bfloat16),
            pltpu.VMEM((n_row, cap1, width), jnp.bfloat16),
            pltpu.VMEM((NIRREP, cap1, steps * local_k), jnp.bfloat16),
            pltpu.VMEM((NIRREP, cap2, n_row * cap1), jnp.bfloat16),
            pltpu.SemaphoreType.DMA((n_row,)),
            pltpu.SemaphoreType.DMA((n_row,)),
            pltpu.SemaphoreType.DMA((n_row,)),
        ],
        compiler_params=pltpu.CompilerParams(
            vmem_limit_bytes=24 * MIB, collective_id=1, has_side_effects=True
        ),
    )(irrep_blk, slot1, slot2, integrals)


def per_device(n_row, n_col, amplitudes, integrals, pair_irrep, block_offset, residual):
    steps, local_k, ab_local = integrals.shape
    n1 = steps * local_k
    cap1 = round_up(-(-n1 // 3), 16)
    cap2 = round_up(-(-n1 * n_row // 6), 16)
    tight = cap2 - 16
    row, col = lax.axis_index("row"), lax.axis_index("col")

    pairs = np.arange(steps * local_k * n_row)
    holder = pairs // local_k % n_row
    same = holder[:, None] == holder[None, :]
    within = same & (pairs[:, None] <= pairs[None, :])
    ahead = holder[:, None] < holder[None, :]
    rows = np.arange(n_row)
    held = holder[:, None] == rows[None, :]
    before = holder[:, None] < rows[None, :]
    tally = np.concatenate([within, within | ahead, held, before], axis=1)
    mine = pair_irrep.reshape(1, -1) == lax.iota(jnp.int32, NIRREP)[:, None]
    sums = jnp.dot(
        mine.astype(jnp.bfloat16), jnp.asarray(tally, jnp.bfloat16),
        preferred_element_type=jnp.float32,
    ).astype(jnp.int32)
    depth = pairs.size
    rank = jnp.where(mine, sums[:, :depth] - 1, -1).reshape(NIRREP, steps, n_row, local_k)
    slot3 = jnp.where(mine, sums[:, depth:2 * depth] - 1, -1)
    count = sums[:, 2 * depth:2 * depth + n_row]
    base = sums[:, 2 * depth + n_row:]
    upto = base + count
    most = jnp.max(upto)
    level = jnp.where(
        jnp.max(count) > cap1, 2, (most > tight).astype(jnp.int32) + (most > cap2).astype(jnp.int32)
    )

    slot1 = lax.dynamic_index_in_dim(rank, row, axis=2, keepdims=False).reshape(NIRREP, n1)
    spot = lax.iota(jnp.int32, cap1)
    slot2 = jnp.where(spot[None, None] < count[:, :, None], base[:, :, None] + spot, -1)
    slot2 = slot2.reshape(NIRREP, n_row * cap1)

    blocks = n_col * ab_local // GRAIN
    starts = lax.iota(jnp.int32, blocks) * GRAIN
    irrep_blk = jnp.sum((starts[:, None] >= block_offset[None, 1:-1]).astype(jnp.int32), axis=1)

    per_col = ab_local // GRAIN

    def by_links(amplitudes, integrals, residual):
        mine = exchange(integrals, slot1, slot2, irrep_blk, cap1, tight, n_row)
        amp = amplitudes.reshape(amplitudes.shape[0], -1)
        return spread_add(amp, slot3, irrep_blk, mine, residual, n_row, n_col)

    def sparse(amplitudes, integrals, residual):
        mine1 = pack(integrals, slot1, irrep_blk, col * per_col, cap1, n_row)
        ours = lax.all_to_all(mine1, "row", split_axis=0, concat_axis=0, tiled=True)
        ours = ours.reshape(n_row * cap1, ab_local // n_row)
        first = col * per_col + row * (per_col // n_row)
        mine2 = pack(ours, slot2, irrep_blk, first, cap2, 1)
        packed = lax.all_gather(mine2, ("row", "col"), axis=0, tiled=True)
        amp = amplitudes.reshape(amplitudes.shape[0], -1)
        return ladder_add(amp, slot3, irrep_blk, packed, residual, n_row, n_col)

    def full(amplitudes, integrals, residual):
        return dense(amplitudes, integrals, pair_irrep, block_offset, residual)

    quick = by_links if (n_row, n_col) == (8, 4) else sparse
    return lax.switch(level, [quick, sparse, full], amplitudes, integrals, residual)


def solution(mesh):
    in_specs = (
        P(("row", "col"), None, None),
        P(None, "row", "col"),
        P(),
        P(),
        P(("row", "col"), None),
    )
    out_specs = P(("row", "col"), None)
    body = functools.partial(per_device, mesh.shape["row"], mesh.shape["col"])
    return jax.shard_map(
        body, mesh=mesh, in_specs=in_specs, out_specs=out_specs, check_vma=False
    )
```
